128 devices in a mesh: row: 16 (over y, x), col: 8 (over z, core).
Axes of the slice: x: 4, y: 4, z: 4, core: 2. Of those that a mesh axis runs over, the one named last changes fastest.
Arguments:
- basis_values: bfloat16 [196608, 2048], P(('row', 'col')), may hold values from -6 to 6
- point_weights: float32 [196608], P(('row', 'col')), may hold values from 0.005 to 0.05
- density_stored: bfloat16 [16384, 16384], P('row', 'col'), may hold values from -0.0029907227 to 0.0029907227
- relevant_blocks: int32 [128, 16], replicated, may hold values from 0 to 127, as said below
- relevant_count: int32 [128], replicated, may hold values from 8 to 16, as said below
- block_home: int32 [128], replicated, may hold values from 0 to 127, as said below
Outputs:
- potential_matrix: float32 [16384, 16384], P('row', 'col')
The draws below stay inside these ranges and needn't reach their ends.
Inputs may be any that keep to these rules, and one draw needn't show every extreme that they name: `relevant_blocks`: A group's list, in order, names blocks whose stored positions are s, s + 1, s + 2, ... modulo 128 for some start s of that group, over all 16 entries; only the first relevant_count[d] are live. So a group's live entries fall at most 1 to one residue class modulo 16 and at most 2 to one modulo 8, and some group reaches both in every draw. `relevant_count`: some group has 16 live entries and some has 8. `block_home`: A permutation of the stored positions.
All inputs are finite; a program needn't handle non-finite values.
Results may differ from the reference program's by a relative error of at most 0.0029.
Values may be sent and summed in bfloat16 or wider, within the bound.
A program may use at most 128 MiB of HBM per device.

```python
import math
import jax
import jax.numpy as jnp
from jax import lax

BLOCK_FUNCTIONS = 128
MAX_RELEVANT = 16
BR = 8
GROUPS = 128
ROWS = 1536
POINTS = 196608
NBLK = 128
BC = 16
FUNCS = 16384
N_ROW = 16
N_COL = 8


def list_tables(key):
    home_key = jax.random.fold_in(key, 11)
    start_key = jax.random.fold_in(key, 23)
    count_key = jax.random.fold_in(key, 37)
    home = jax.random.permutation(home_key, NBLK).astype(jnp.int32)
    owner_of = jnp.zeros((NBLK,), jnp.int32).at[home].set(jnp.arange(NBLK, dtype=jnp.int32))
    starts = jax.random.randint(start_key, (GROUPS,), 0, NBLK).astype(jnp.int32)
    counts = jax.random.randint(count_key, (GROUPS,), MAX_RELEVANT // 2, MAX_RELEVANT + 1).astype(jnp.int32)
    counts = counts.at[0].set(MAX_RELEVANT).at[1].set(MAX_RELEVANT // 2)
    spots = (starts[:, None] + jnp.arange(MAX_RELEVANT, dtype=jnp.int32)[None, :]) % NBLK
    lists = owner_of[spots]
    return (home, lists, counts)


def draw_relevant_blocks(key, part):
    return list_tables(key)[1]


def draw_relevant_count(key, part):
    return list_tables(key)[2]


def draw_block_home(key, part):
    return list_tables(key)[0]


def block_scale(rng, shape, cuts, least, largest):
    factor_of = 1.0
    for axis_at, blocks in cuts:
        heights = jax.random.uniform(jax.random.fold_in(jax.random.fold_in(rng, 6), axis_at), (blocks,), jnp.float32, least / len(cuts), largest / len(cuts))
        factor_of = factor_of * jnp.repeat(jnp.exp(heights), shape[axis_at] // blocks).reshape((-1,) + (1,) * (len(shape) - 1 - axis_at))
    return factor_of


def normal_values(stream_key, dims, width, bound, split=(), kind=jnp.bfloat16):
    drawn = jax.random.normal(stream_key, dims, jnp.float32) * width
    if len(split) > 0:
        drawn = block_scale(stream_key, dims, split, -0.22, 0.18) * drawn
    return jnp.clip(drawn, min=-bound, max=bound).astype(kind)


def setup_inputs(seed: int = 0) -> dict:
    streams_of = jax.random.split(jax.random.key(seed), 7)
    basis_values = normal_values(streams_of[0], (POINTS, MAX_RELEVANT * BLOCK_FUNCTIONS), 1.0, 6.0, ((0, 128),))
    point_weights = jnp.clip(jnp.exp(math.log(0.05) - 2.3025851 * jax.random.uniform(streams_of[1], (POINTS,), jnp.float32) ** block_scale(streams_of[1], (POINTS,), ((0, 128),), -0.2, 0.2)), 0.005, 0.05)
    density_stored = normal_values(streams_of[2], (FUNCS, FUNCS), 0.0005, 0.0029907227, ((0, 16), (1, 8)))
    relevant_blocks = draw_relevant_blocks(jax.random.fold_in(streams_of[6], 71), 0)
    relevant_count = draw_relevant_count(jax.random.fold_in(streams_of[6], 71), 0)
    block_home = draw_block_home(jax.random.fold_in(streams_of[6], 71), 0)
    return dict(basis_values=basis_values, point_weights=point_weights, density_stored=density_stored, relevant_blocks=relevant_blocks, relevant_count=relevant_count, block_home=block_home)


def reference(basis_values, point_weights, density_stored, relevant_blocks, relevant_count, block_home):
    full_width = MAX_RELEVANT * BLOCK_FUNCTIONS
    stored = density_stored.reshape(NBLK, BLOCK_FUNCTIONS, NBLK, BLOCK_FUNCTIONS).transpose(0, 2, 1, 3)
    positions = block_home[relevant_blocks]
    row_index = ((positions % N_ROW) * BR + positions // N_ROW).astype(jnp.int32)
    col_index = ((positions % N_COL) * BC + positions // N_COL).astype(jnp.int32)
    basis = basis_values.reshape(GROUPS, ROWS, full_width)
    weights = point_weights.reshape(GROUPS, ROWS)
    slot_ids = jnp.arange(MAX_RELEVANT, dtype=jnp.int32)

    def group_step(total, inputs):
        phi_raw, weight_row, count, rows_at, cols_at = inputs
        live = jnp.repeat(slot_ids < count, BLOCK_FUNCTIONS)
        orbital_values = jnp.where(live[None, :], phi_raw, jnp.zeros((), phi_raw.dtype))
        sub = stored[rows_at[:, None], cols_at[None, :]]
        sub = sub.transpose(0, 2, 1, 3).reshape(full_width, full_width)
        dens = jnp.dot(orbital_values, sub, preferred_element_type=jnp.float32)
        rho = jnp.sum(dens * orbital_values.astype(jnp.float32), axis=1)
        pot = weight_row * rho * (1.0 + rho * rho) ** (-1.0 / 3.0)
        weighted_orbitals = (orbital_values.astype(jnp.float32) * pot[:, None]).astype(orbital_values.dtype)
        potential_submatrix = jnp.dot(orbital_values.T, weighted_orbitals, preferred_element_type=jnp.float32)
        potential_blocks = potential_submatrix.reshape(MAX_RELEVANT, BLOCK_FUNCTIONS, MAX_RELEVANT, BLOCK_FUNCTIONS).transpose(0, 2, 1, 3)
        total = total.at[rows_at[:, None], cols_at[None, :]].add(potential_blocks)
        return total, None

    zeros = jnp.zeros((NBLK, NBLK, BLOCK_FUNCTIONS, BLOCK_FUNCTIONS), jnp.float32)
    total, _ = lax.scan(group_step, zeros, (basis, weights, relevant_count, row_index, col_index))
    return total.transpose(0, 2, 1, 3).reshape(NBLK * BLOCK_FUNCTIONS, NBLK * BLOCK_FUNCTIONS)
```

```python
import functools

import jax
import jax.numpy as jnp
from jax import lax
from jax.experimental import pallas as pl
from jax.experimental.pallas import tpu as pltpu
from jax.sharding import PartitionSpec as P

MESH = pl.DeviceIdType.MESH
NROW, NCOL, GROUPS, B = 16, 8, 128, 128
ENTRIES = 16
ROWS = 1536
WIDTH = ENTRIES * B


def place(residue):
    return (residue % NCOL) * 2 + residue // NCOL


def offset_target(step, row, col):
    t = (step * (step + 1) // 2) % GROUPS
    y = (row // 4 + t % 4) % 4
    x = (row % 4 + (t // 4) % 4) % 4
    z = (col // 2 + (t // 16) % 4) % 4
    core = (col + t // 64) % 2
    return y * 4 + x, z * 2 + core


def position(start, residue, period):
    return (start + ((residue - start) & (ENTRIES - 1))) & (GROUPS - 1)


def group_kernel(
    start_ref, cnt_ref, w_ref, dens_hbm, phi_hbm, out_ref,
    dens_ref, phi_ref, scaled_ref, phit_ref, sub_ref, stage_ref, rho_ref, pot_ref,
    dens_sem, phi_sem, dsend, drecv, vsend, vrecv, self_sem,
):
    row, col = lax.axis_index("row"), lax.axis_index("col")
    me = row * NCOL + col

    def column(k):
        return pl.ds(k * B, B)

    dens_copies = [
        pltpu.make_async_copy(dens_hbm.at[:, :, column(k)], dens_ref.at[k], dens_sem) for k in range(ENTRIES)
    ]
    phi_copies = [
        pltpu.make_async_copy(phi_hbm.at[:, column(k)], phi_ref.at[k], phi_sem) for k in range(ENTRIES)
    ]
    for copy in dens_copies + phi_copies:
        copy.start()

    barrier = pltpu.get_barrier_semaphore()

    def greet(i, carry):
        r, c = offset_target(i, row, col)
        pl.semaphore_signal(barrier, inc=1, device_id=(r, c), device_id_type=MESH)
        return carry

    lax.fori_loop(1, GROUPS, greet, 0)

    def pick(r, c):
        start = start_ref[r * NCOL + c]
        i = position(start, row, NROW) >> 4
        j0 = position(start, col, ENTRIES) >> 3
        j1 = position(start, col + NCOL, ENTRIES) >> 3
        return dens_ref[j0, i], dens_ref[j1, i]

    def slot(r, c):
        return pl.multiple_of((c * ENTRIES + place(r)) * B, B)

    pltpu.make_async_copy(dens_ref, dens_ref, dens_sem).wait()

    def prepare(i, carry):
        r, c = offset_target(i, row, col)
        left, right = pick(r, c)
        at = slot(r, c)
        stage_ref[pl.ds(at, B), pl.ds(0, B)] = left
        stage_ref[pl.ds(at, B), pl.ds(B, B)] = right
        return carry

    lax.fori_loop(1, GROUPS, prepare, 0)
    my_rows = pl.ds(pl.multiple_of(place(row) * B, B), B)
    my_cols = pl.ds(pl.multiple_of(col * 2 * B, B), 2 * B)
    left, right = pick(row, col)
    sub_ref[my_rows, my_cols] = jnp.concatenate([left, right], axis=1)

    pl.semaphore_wait(barrier, GROUPS - 1)

    def send(i, carry):
        r, c = offset_target(i, row, col)
        pltpu.make_async_remote_copy(
            src_ref=stage_ref.at[pl.ds(slot(r, c), B)],
            dst_ref=sub_ref.at[my_rows, my_cols],
            send_sem=dsend, recv_sem=drecv,
            device_id=(r, c), device_id_type=MESH,
        ).start()
        return carry

    lax.fori_loop(1, GROUPS, send, 0)

    pltpu.make_async_copy(phi_ref, phi_ref, phi_sem).wait()
    my_start = start_ref[me]
    my_count = cnt_ref[me]

    def turn(at, carry):
        residue = at // 2 + (at % 2) * NCOL
        k = (residue - my_start) & (ENTRIES - 1)
        live = jnp.clip(my_count - k, 0, 1).astype(jnp.float32)
        for t in range(ROWS // B):
            tile = phi_ref[k, pl.ds(t * B, B), :]
            tile = (tile.astype(jnp.float32) * live).T
            phit_ref[pl.ds(pl.multiple_of(at * B, B), B), pl.ds(t * B, B)] = tile.astype(jnp.bfloat16)
        return carry

    lax.fori_loop(0, ENTRIES, turn, 0)
    rho_ref[...] = jnp.zeros_like(rho_ref)

    everything = stage_ref.at[pl.ds(0, (GROUPS - 1) * B)]
    pltpu.make_async_copy(everything, everything, drecv).wait()

    M, N = 512, 256

    def density(step, carry):
        rows = pl.ds(pl.multiple_of((step % (WIDTH // M)) * M, M), M)
        cols = pl.ds(pl.multiple_of((step // (WIDTH // M)) * N, N), N)
        g = jnp.dot(sub_ref[rows, :], phit_ref[:, cols], preferred_element_type=jnp.float32)
        g = g * phit_ref[rows, cols].astype(jnp.float32)
        rho_ref[:, cols] += jnp.sum(g.reshape(M // 8, 8, N), axis=0)
        return carry

    lax.fori_loop(0, (WIDTH // M) * (ROWS // N), density, 0)

    rho = jnp.sum(rho_ref[...], axis=0, keepdims=True)
    pot_ref[...] = w_ref[...] * rho * jnp.exp(jnp.log(1.0 + rho * rho) * (-1.0 / 3.0))

    pltpu.make_async_copy(everything, everything, dsend).wait()

    def potential(i, carry):
        c = (col + i) % NCOL
        cols = pl.ds(pl.multiple_of(c * 2 * B, 2 * B), 2 * B)
        scaled_ref[...] = (
            phit_ref[cols, :].astype(jnp.float32) * pot_ref[...]
        ).astype(jnp.bfloat16)

        def part(j, carry):
            m = (row % 4 + j) % 4
            rows = pl.ds(pl.multiple_of(m * M, M), M)
            v = lax.dot_general(
                phit_ref[rows, :], scaled_ref[...],
                (((1,), (1,)), ((), ())), preferred_element_type=jnp.float32,
            )
            base = pl.multiple_of((c * ENTRIES + m * 4) * B, B)
            stage_ref[pl.ds(base, M)] = v.astype(jnp.bfloat16)
            for n in range(4):
                at = m * 4 + n
                r = at // 2 + (at % 2) * NCOL
                source = stage_ref.at[pl.ds(pl.multiple_of(base + n * B, B), B)]

                @pl.when(r * NCOL + c != me)
                def _():
                    pltpu.make_async_remote_copy(
                        src_ref=source, dst_ref=out_ref.at[me],
                        send_sem=vsend, recv_sem=vrecv,
                        device_id=(r, c), device_id_type=MESH,
                    ).start()

            return carry

        return lax.fori_loop(0, 4, part, carry)

    lax.fori_loop(0, NCOL, potential, 0)
    own = pltpu.make_async_copy(stage_ref.at[pl.ds(slot(row, col), B)], out_ref.at[me], self_sem)
    own.start()
    own.wait()
    pltpu.make_async_copy(everything, everything, vsend).wait()
    pltpu.make_async_copy(everything, everything, vrecv).wait()


def exchange(starts, cnt, w, dens, phi):
    vmem = pl.BlockSpec(memory_space=pltpu.VMEM)
    smem = pl.BlockSpec(memory_space=pltpu.SMEM)
    hbm = pl.BlockSpec(memory_space=pl.ANY)
    return pl.pallas_call(
        group_kernel,
        out_shape=jax.ShapeDtypeStruct((GROUPS, B, 2 * B), jnp.bfloat16),
        in_specs=[smem, smem, vmem, hbm, hbm],
        out_specs=hbm,
        scratch_shapes=[
            pltpu.VMEM((ENTRIES, 8, B, B), jnp.bfloat16),
            pltpu.VMEM((ENTRIES, ROWS, B), jnp.bfloat16),
            pltpu.VMEM((2 * B, ROWS), jnp.bfloat16),
            pltpu.VMEM((WIDTH, ROWS), jnp.bfloat16),
            pltpu.VMEM((WIDTH, WIDTH), jnp.bfloat16),
            pltpu.VMEM((GROUPS * B, 2 * B), jnp.bfloat16),
            pltpu.VMEM((8, ROWS), jnp.float32),
            pltpu.VMEM((1, ROWS), jnp.float32),
            pltpu.SemaphoreType.DMA,
            pltpu.SemaphoreType.DMA,
            pltpu.SemaphoreType.DMA,
            pltpu.SemaphoreType.DMA,
            pltpu.SemaphoreType.DMA,
            pltpu.SemaphoreType.DMA,
            pltpu.SemaphoreType.DMA,
        ],
        compiler_params=pltpu.CompilerParams(
            collective_id=0, has_side_effects=True, vmem_limit_bytes=56 << 20
        ),
        cost_estimate=pl.CostEstimate(flops=4 * ROWS * WIDTH * WIDTH, bytes_accessed=32 << 20, transcendentals=2 * ROWS),
    )(starts, cnt, w, dens, phi)


CHUNK = 8


def sum_kernel(where_ref, start_ref, parts_ref, out_ref):
    row, col = where_ref[0], where_ref[1]
    step = pl.program_id(0)

    @pl.when(step == 0)
    def _():
        out_ref[...] = jnp.zeros_like(out_ref)

    for n in range(CHUNK):
        start = start_ref[step * CHUNK + n]
        i = position(start, row, NROW) // NROW
        rows = pl.ds(pl.multiple_of(i * B, B), B)
        for h in range(2):
            j = position(start, col + h * NCOL, ENTRIES) // NCOL
            cols = pl.ds(pl.multiple_of(j * B, B), B)
            out_ref[rows, cols] += parts_ref[n, :, pl.ds(h * B, B)].astype(jnp.float32)


def collect(where, starts, parts):
    smem = pl.BlockSpec(memory_space=pltpu.SMEM)
    return pl.pallas_call(
        sum_kernel,
        grid=(GROUPS // CHUNK,),
        out_shape=jax.ShapeDtypeStruct((1024, WIDTH), jnp.float32),
        in_specs=[smem, smem, pl.BlockSpec((CHUNK, B, 2 * B), lambda g: (g, 0, 0))],
        out_specs=pl.BlockSpec((1024, WIDTH), lambda g: (0, 0)),
        compiler_params=pltpu.CompilerParams(vmem_limit_bytes=40 << 20),
    )(where, starts, parts)


def body(basis_values, point_weights, density_stored, relevant_blocks, relevant_count, block_home):
    starts = block_home[relevant_blocks[:, 0]]
    parts = exchange(
        starts, relevant_count, point_weights.reshape(1, ROWS), density_stored.reshape(8, B, WIDTH), basis_values,
    )
    where = jnp.stack([lax.axis_index("row"), lax.axis_index("col")]).astype(jnp.int32)
    return collect(where, starts, parts)


def solution(mesh):
    in_specs = (P(("row", "col"), None), P(("row", "col")), P("row", "col"), P(), P(), P())
    return jax.shard_map(body, mesh=mesh, in_specs=in_specs, out_specs=P("row", "col"), check_vma=False)
```

```python
import jax
import jax.numpy as jnp
from jax import lax
from jax.experimental import pallas as pl
from jax.experimental.pallas import tpu as pltpu
from jax.sharding import PartitionSpec as P

MESH = pl.DeviceIdType.MESH
NROW, NCOL, GROUPS, B = 16, 8, 128, 128
ENTRIES = 16
ROWS = 1536
WIDTH = ENTRIES * B
BLOCK_ROWS = 8
GATHER_ROUNDS, GATHER_ROWS = 4, 32
RETURN_ROUNDS, RETURN_ROWS = 2, 64


def place(residue):
    return (residue % NCOL) * 2 + residue // NCOL


def offset_target(step, row, col):
    t = (step * (step + 1) // 2) % GROUPS
    y = (row // 4 + t % 4) % 4
    x = (row % 4 + (t // 4) % 4) % 4
    z = (col // 2 + (t // 16) % 4) % 4
    core = (col + t // 64) % 2
    return y * 4 + x, z * 2 + core


def list_place(start, residue):
    return (residue - start) & (ENTRIES - 1)


def position(start, residue):
    return (start + list_place(start, residue)) & (GROUPS - 1)


def lag(row, col):
    return (col - row + NROW) % NCOL


def group_kernel(
    start_ref, cnt_ref, w_ref, dens_hbm, phi_hbm, main_ref, far_ref,
    dens_ref, phi_ref, scaled_ref, phit_ref, sub_ref, stage_ref, back_ref, rho_ref, pot_ref,
    dens_sem, phi_sem, dsend, drecv, msend, mrecv, fsend, frecv, self_sem,
):
    row, col = lax.axis_index("row"), lax.axis_index("col")
    me = row * NCOL + col

    def column(k):
        return pl.ds(k * B, B)

    dens_copies = [
        pltpu.make_async_copy(dens_hbm.at[:, :, column(k)], dens_ref.at[k], dens_sem) for k in range(ENTRIES)
    ]
    phi_copies = [
        pltpu.make_async_copy(phi_hbm.at[:, column(k)], phi_ref.at[k], phi_sem) for k in range(ENTRIES)
    ]
    for copy in dens_copies + phi_copies:
        copy.start()

    barrier = pltpu.get_barrier_semaphore()

    def greet(i, carry):
        r, c = offset_target(i, row, col)
        pl.semaphore_signal(barrier, inc=1, device_id=(r, c), device_id_type=MESH)
        return carry

    lax.fori_loop(1, GROUPS, greet, 0)

    def pick(r, c):
        start = start_ref[r * NCOL + c]
        i = position(start, row) >> 4
        j0 = position(start, col) >> 3
        j1 = position(start, col + NCOL) >> 3
        return dens_ref[j0, i], dens_ref[j1, i]

    pltpu.make_async_copy(dens_ref, dens_ref, dens_sem).wait()

    def staged(n, r, c):
        at = (n * GROUPS + r * NCOL + c) * GATHER_ROWS
        return pl.ds(pl.multiple_of(at, GATHER_ROWS), GATHER_ROWS)

    def prepare(i, carry):
        r, c = offset_target(i, row, col)
        left, right = pick(r, c)
        for n in range(GATHER_ROUNDS):
            part = slice(n * GATHER_ROWS, (n + 1) * GATHER_ROWS)
            stage_ref[staged(n, r, c), pl.ds(0, B)] = left[part]
            stage_ref[staged(n, r, c), pl.ds(B, B)] = right[part]
        return carry

    lax.fori_loop(1, GROUPS, prepare, 0)
    my_rows = pl.ds(pl.multiple_of(place(row) * GATHER_ROWS, GATHER_ROWS), GATHER_ROWS)
    my_cols = pl.ds(pl.multiple_of(col * 2 * B, B), 2 * B)
    left, right = pick(row, col)
    for n in range(GATHER_ROUNDS):
        part = slice(n * GATHER_ROWS, (n + 1) * GATHER_ROWS)
        sub_ref[n, my_rows, my_cols] = jnp.concatenate([left[part], right[part]], axis=1)

    pl.semaphore_wait(barrier, GROUPS - 1)

    def send_round(n, carry):
        def send(i, carry):
            r, c = offset_target(i, row, col)
            pltpu.make_async_remote_copy(
                src_ref=stage_ref.at[staged(n, r, c)],
                dst_ref=sub_ref.at[n, my_rows, my_cols],
                send_sem=dsend, recv_sem=drecv.at[n],
                device_id=(r, c), device_id_type=MESH,
            ).start()
            return carry

        return lax.fori_loop(1, GROUPS, send, carry)

    lax.fori_loop(0, GATHER_ROUNDS, send_round, 0)

    pltpu.make_async_copy(phi_ref, phi_ref, phi_sem).wait()
    my_start = start_ref[me]
    my_count = cnt_ref[me]

    def turn(at, carry):
        residue = at // 2 + (at % 2) * NCOL
        k = list_place(my_start, residue)
        live = jnp.clip(my_count - k, 0, 1).astype(jnp.float32)
        for t in range(ROWS // B):
            tile = phi_ref[k, pl.ds(t * B, B), :]
            tile = (tile.astype(jnp.float32) * live).T
            phit_ref[at, :, pl.ds(t * B, B)] = tile.astype(jnp.bfloat16)
        return carry

    lax.fori_loop(0, ENTRIES, turn, 0)
    rho_ref[...] = jnp.zeros_like(rho_ref)

    M, N = ENTRIES * GATHER_ROWS, 256
    one_round = stage_ref.at[pl.ds(0, (GROUPS - 1) * GATHER_ROWS)]

    def density_round(n, carry):
        pltpu.make_async_copy(one_round, one_round, drecv.at[n]).wait()
        rows = pl.ds(pl.multiple_of(n * GATHER_ROWS, GATHER_ROWS), GATHER_ROWS)

        def density(step, carry):
            cols = pl.ds(pl.multiple_of(step * N, N), N)
            g = jnp.dot(
                sub_ref[n], phit_ref[:, :, cols].reshape(WIDTH, N), preferred_element_type=jnp.float32
            )
            g = g * phit_ref[:, rows, cols].reshape(M, N).astype(jnp.float32)
            rho_ref[:, cols] += jnp.sum(g.reshape(M // 8, 8, N), axis=0)
            return carry

        return lax.fori_loop(0, ROWS // N, density, carry)

    lax.fori_loop(0, GATHER_ROUNDS, density_round, 0)

    rho = jnp.sum(rho_ref[...], axis=0, keepdims=True)
    pot_ref[...] = w_ref[...] * rho * jnp.exp(jnp.log(1.0 + rho * rho) * (-1.0 / 3.0))

    def weigh(c, carry):
        scaled_ref[c] = (
            phit_ref[pl.ds(c * 2, 2)].reshape(2 * B, ROWS).astype(jnp.float32) * pot_ref[...]
        ).astype(jnp.bfloat16)
        return carry

    lax.fori_loop(0, NCOL, weigh, 0)

    HALF = ENTRIES // 2

    def return_round(n, carry):
        rows = pl.ds(pl.multiple_of(n * RETURN_ROWS, RETURN_ROWS), RETURN_ROWS)

        def potential(step, carry):
            c, half = step // 2, step % 2
            v = lax.dot_general(
                phit_ref[pl.ds(half * HALF, HALF), rows, :].reshape(HALF * RETURN_ROWS, ROWS), scaled_ref[c],
                (((1,), (1,)), ((), ())), preferred_element_type=jnp.float32,
            ).astype(jnp.bfloat16).reshape(HALF, RETURN_ROWS, 2 * B)
            back_ref[n, c * 2, pl.ds(half * HALF, HALF)] = v[:, :, :B]
            back_ref[n, c * 2 + 1, pl.ds(half * HALF, HALF)] = v[:, :, B:]
            return carry

        lax.fori_loop(0, NCOL * 2, potential, 0)

        def main_copy(r, c):
            residue = (r + lag(r, c)) % NROW
            return pltpu.make_async_remote_copy(
                src_ref=back_ref.at[n, place(residue), place(r)],
                dst_ref=main_ref.at[n, me],
                send_sem=msend, recv_sem=mrecv,
                device_id=(r, c), device_id_type=MESH,
            )

        def far_copy(r, c):
            residue = (r + NCOL) % NROW
            return pltpu.make_async_remote_copy(
                src_ref=back_ref.at[n, place(residue), place(r)],
                dst_ref=far_ref.at[n, me],
                send_sem=fsend, recv_sem=frecv,
                device_id=(r, c), device_id_type=MESH,
            )

        def give(i, carry):
            r, c = offset_target(i, row, col)
            main_copy(r, c).start()

            @pl.when(lag(r, c) == 0)
            def _():
                far_copy(r, c).start()

            return carry

        lax.fori_loop(1, GROUPS, give, 0)
        residue = (row + lag(row, col)) % NROW
        own = pltpu.make_async_copy(back_ref.at[n, place(residue), place(row)], main_ref.at[n, me], self_sem)
        own.start()
        own.wait()

        @pl.when(lag(row, col) == 0)
        def _():
            residue = (row + NCOL) % NROW
            own = pltpu.make_async_copy(back_ref.at[n, place(residue), place(row)], far_ref.at[n, me], self_sem)
            own.start()
            own.wait()

        return carry

    lax.fori_loop(0, RETURN_ROUNDS, return_round, 0)

    every_block = stage_ref.at[pl.ds(0, (GROUPS - 1) * B // 2)]
    pltpu.make_async_copy(stage_ref.at[pl.ds(0, (GROUPS - 1) * B)], stage_ref.at[pl.ds(0, (GROUPS - 1) * B)], dsend).wait()
    pltpu.make_async_copy(every_block, every_block, msend).wait()
    pltpu.make_async_copy(every_block, every_block, mrecv).wait()

    @pl.when(lag(row, col) == 0)
    def _():
        others = stage_ref.at[pl.ds(0, (NROW - 1) * B // 2)]
        pltpu.make_async_copy(others, others, fsend).wait()
        pltpu.make_async_copy(every_block, every_block, frecv).wait()

    @pl.when(lag(row, col) != 0)
    def _():
        others = stage_ref.at[pl.ds(0, NROW * B // 2)]
        pltpu.make_async_copy(others, others, fsend).wait()


VMEM = pl.BlockSpec(memory_space=pltpu.VMEM)
SMEM = pl.BlockSpec(memory_space=pltpu.SMEM)
HBM = pl.BlockSpec(memory_space=pl.ANY)


def exchange(starts, cnt, w, dens, phi):
    parts = jax.ShapeDtypeStruct((RETURN_ROUNDS, GROUPS, RETURN_ROWS, B), jnp.bfloat16)
    return pl.pallas_call(
        group_kernel,
        out_shape=[parts, parts],
        in_specs=[SMEM, SMEM, VMEM, HBM, HBM],
        out_specs=[HBM, HBM],
        scratch_shapes=[
            pltpu.VMEM((ENTRIES, BLOCK_ROWS, B, B), jnp.bfloat16),
            pltpu.VMEM((ENTRIES, ROWS, B), jnp.bfloat16),
            pltpu.VMEM((NCOL, 2 * B, ROWS), jnp.bfloat16),
            pltpu.VMEM((ENTRIES, B, ROWS), jnp.bfloat16),
            pltpu.VMEM((GATHER_ROUNDS, ENTRIES * GATHER_ROWS, WIDTH), jnp.bfloat16),
            pltpu.VMEM((GROUPS * B, 2 * B), jnp.bfloat16),
            pltpu.VMEM((RETURN_ROUNDS, ENTRIES, ENTRIES, RETURN_ROWS, B), jnp.bfloat16),
            pltpu.VMEM((8, ROWS), jnp.float32),
            pltpu.VMEM((1, ROWS), jnp.float32),
            pltpu.SemaphoreType.DMA,
            pltpu.SemaphoreType.DMA,
            pltpu.SemaphoreType.DMA,
            pltpu.SemaphoreType.DMA((GATHER_ROUNDS,)),
            pltpu.SemaphoreType.DMA,
            pltpu.SemaphoreType.DMA,
            pltpu.SemaphoreType.DMA,
            pltpu.SemaphoreType.DMA,
            pltpu.SemaphoreType.DMA,
        ],
        compiler_params=pltpu.CompilerParams(
            collective_id=0, has_side_effects=True, vmem_limit_bytes=60 << 20
        ),
        cost_estimate=pl.CostEstimate(flops=4 * ROWS * WIDTH * WIDTH, bytes_accessed=32 << 20, transcendentals=2 * ROWS),
    )(starts, cnt, w, dens, phi)


CHUNK = 16


def sum_kernel(where_ref, start_ref, main_ref, far_ref, near_ref, wide_ref, turned_ref):
    row, col = where_ref[0], where_ref[1]
    n, step = pl.program_id(0), pl.program_id(1)
    shift = lag(row, col)
    rows = pl.ds(pl.multiple_of(n * RETURN_ROWS, RETURN_ROWS), RETURN_ROWS)

    @pl.when(step == 0)
    def _():
        near_ref[:, rows, :] = jnp.zeros((2 * BLOCK_ROWS, RETURN_ROWS, B), jnp.float32)
        wide_ref[:, rows, :] = jnp.zeros((2 * BLOCK_ROWS, RETURN_ROWS, B), jnp.float32)

    def slot(start, apart):
        k, l = list_place(start, row), list_place(start, row + apart)
        i = ((start + k) & (GROUPS - 1)) >> 4
        return i * 2 + (l < k).astype(jnp.int32)

    for m in range(CHUNK):
        at = slot(start_ref[step * CHUNK + m], shift)
        near_ref[at, rows, :] += main_ref[0, m].astype(jnp.float32)

    @pl.when(shift == 0)
    def _():
        for m in range(CHUNK):
            at = slot(start_ref[step * CHUNK + m], NCOL)
            wide_ref[at, rows, :] += far_ref[0, m].astype(jnp.float32)

    @pl.when((n == RETURN_ROUNDS - 1) & (step == GROUPS // CHUNK - 1))
    def _():
        for at in range(2 * BLOCK_ROWS):
            turned_ref[at] = near_ref[at].T.astype(jnp.bfloat16)


def collect(where, starts, main, far):
    def far_index(n, g, where_ref, start_ref):
        busy = (lag(where_ref[0], where_ref[1]) == 0).astype(jnp.int32)
        return n * busy, g * busy, 0, 0

    parts = (1, CHUNK, RETURN_ROWS, B)
    sums = (2 * BLOCK_ROWS, B, B)
    return pl.pallas_call(
        sum_kernel,
        grid_spec=pltpu.PrefetchScalarGridSpec(
            num_scalar_prefetch=2,
            grid=(RETURN_ROUNDS, GROUPS // CHUNK),
            in_specs=[
                pl.BlockSpec(parts, lambda n, g, where_ref, start_ref: (n, g, 0, 0)),
                pl.BlockSpec(parts, far_index),
            ],
            out_specs=[pl.BlockSpec(sums, lambda n, g, where_ref, start_ref: (0, 0, 0))] * 3,
        ),
        out_shape=[
            jax.ShapeDtypeStruct(sums, jnp.float32),
            jax.ShapeDtypeStruct(sums, jnp.float32),
            jax.ShapeDtypeStruct(sums, jnp.bfloat16),
        ],
        compiler_params=pltpu.CompilerParams(vmem_limit_bytes=40 << 20),
    )(where, starts, main, far)


SLOTS = 2 * BLOCK_ROWS


def relay_shift(i):
    return (5 * i + 1) % NROW, (3 * i) % NCOL


def mirror_owner(row, col):
    shift = lag(row, col)
    return (row + shift + NCOL * (shift == 0).astype(jnp.int32)) % NROW, row % NCOL


def mirror_source(row, col):
    return (row + lag(row, col) + NCOL) % NROW, row % NCOL


def mirror_kernel(turned_ref, out_ref, relay_ref, send1, recv1, send2, recv2):
    row, col = lax.axis_index("row"), lax.axis_index("col")
    me = row * NCOL + col

    def relay(i):
        dr, dc = relay_shift(i)
        return (row + dr) % NROW, (col + dc) % NCOL

    def origin(i):
        dr, dc = relay_shift(i)
        return (row - dr + NROW) % NROW, (col - dc + NCOL) % NCOL

    def final(i):
        return mirror_owner(*origin(i))

    barrier = pltpu.get_barrier_semaphore()
    source = mirror_source(row, col)
    expected = SLOTS
    for i in range(SLOTS):
        pl.semaphore_signal(barrier, inc=1, device_id=origin(i), device_id_type=MESH)
        dr, dc = relay_shift(i)
        r, c = (source[0] + dr) % NROW, (source[1] + dc) % NCOL

        @pl.when(r * NCOL + c != me)
        def _():
            pl.semaphore_signal(barrier, inc=1, device_id=(r, c), device_id_type=MESH)

        r, c = final(i)
        expected = expected + (r * NCOL + c != me).astype(jnp.int32)
    pl.semaphore_wait(barrier, expected)

    def first(i):
        return pltpu.make_async_remote_copy(
            src_ref=turned_ref.at[i], dst_ref=relay_ref.at[i], send_sem=send1.at[i], recv_sem=recv1.at[i],
            device_id=relay(i), device_id_type=MESH,
        )

    def second(i):
        return pltpu.make_async_remote_copy(
            src_ref=relay_ref.at[i], dst_ref=out_ref.at[i], send_sem=send2.at[i], recv_sem=recv2.at[i],
            device_id=final(i), device_id_type=MESH,
        )

    for i in range(SLOTS):
        first(i).start()
    for i in range(SLOTS):
        first(i).wait_recv()
        r, c = final(i)
        stays = r * NCOL + c == me

        @pl.when(jnp.logical_not(stays))
        def _():
            second(i).start()

        @pl.when(stays)
        def _():
            pltpu.make_async_copy(relay_ref.at[i], out_ref.at[i], recv2.at[i]).start()

    for i in range(SLOTS):
        first(i).wait_send()
        second(i).wait_recv()
        r, c = final(i)

        @pl.when(r * NCOL + c != me)
        def _():
            second(i).wait_send()


def mirror(turned):
    return pl.pallas_call(
        mirror_kernel,
        out_shape=jax.ShapeDtypeStruct((SLOTS, B, B), jnp.bfloat16),
        in_specs=[VMEM],
        out_specs=VMEM,
        scratch_shapes=[pltpu.VMEM((SLOTS, B, B), jnp.bfloat16)] + [pltpu.SemaphoreType.DMA((SLOTS,))] * 4,
        compiler_params=pltpu.CompilerParams(collective_id=1, has_side_effects=True),
    )(turned)


def place_kernel(where_ref, near_ref, wide_ref, mirrored_ref, out_ref):
    row, col = where_ref[0], where_ref[1]
    i = pl.program_id(0)
    shift = lag(row, col)
    out_ref[...] = jnp.zeros_like(out_ref)
    p = row + NROW * i

    def columns(q):
        return pl.ds(pl.multiple_of(((q & (GROUPS - 1)) >> 3) * B, B), B)

    @pl.when(shift == 0)
    def _():
        out_ref[:, columns(p)] = near_ref[i * 2]
        for w in range(2):
            out_ref[:, columns(p + NCOL - NROW * w)] = wide_ref[i * 2 + w]

    @pl.when(shift != 0)
    def _():
        for w in range(2):
            out_ref[:, columns(p + shift - NROW * w)] = near_ref[i * 2 + w]
            there = p - (NCOL - shift) + NROW * w
            at = ((there & (GROUPS - 1)) >> 4) * 2 + w
            out_ref[:, columns(there)] = mirrored_ref[at].astype(jnp.float32)


def assemble(where, near, wide, mirrored):
    return pl.pallas_call(
        place_kernel,
        grid=(BLOCK_ROWS,),
        out_shape=jax.ShapeDtypeStruct((BLOCK_ROWS * B, WIDTH), jnp.float32),
        in_specs=[SMEM, VMEM, VMEM, VMEM],
        out_specs=pl.BlockSpec((B, WIDTH), lambda i: (i, 0)),
    )(where, near, wide, mirrored)


def body(basis_values, point_weights, density_stored, relevant_blocks, relevant_count, block_home):
    starts = block_home[relevant_blocks[:, 0]]
    main, far = exchange(
        starts, relevant_count, point_weights.reshape(1, ROWS),
        density_stored.reshape(BLOCK_ROWS, B, WIDTH), basis_values,
    )
    where = jnp.stack([lax.axis_index("row"), lax.axis_index("col")]).astype(jnp.int32)
    near, wide, turned = collect(where, starts, main, far)
    return assemble(where, near, wide, mirror(turned))


def solution(mesh):
    in_specs = (P(("row", "col"), None), P(("row", "col")), P("row", "col"), P(), P(), P())
    return jax.shard_map(body, mesh=mesh, in_specs=in_specs, out_specs=P("row", "col"), check_vma=False)
```

```python
import jax
import jax.numpy as jnp
from jax import lax
from jax.experimental import pallas as pl
from jax.experimental.pallas import tpu as pltpu
from jax.sharding import PartitionSpec as P

MESH = pl.DeviceIdType.MESH
NROW, NCOL, GROUPS, B = 16, 8, 128, 128
ENTRIES = 16
ROWS = 1536
WIDTH = ENTRIES * B
BLOCK_ROWS = 8
GATHER_ROUNDS, GATHER_ROWS = 4, 32
RETURN_ROUNDS, RETURN_ROWS = 2, 64
RUN = 32
SLOTS = 2 * BLOCK_ROWS


def place(residue):
    return (residue % NCOL) * 2 + residue // NCOL


def offset_target(step, row, col):
    t = (step * (step + 1) // 2) % GROUPS
    y = (row // 4 + t % 4) % 4
    x = (row % 4 + (t // 4) % 4) % 4
    z = (col // 2 + (t // 16) % 4) % 4
    core = (col + t // 64) % 2
    return y * 4 + x, z * 2 + core


def list_place(start, residue):
    return (residue - start) & (ENTRIES - 1)


def position(start, residue):
    return (start + list_place(start, residue)) & (GROUPS - 1)


def lag(row, col):
    return (col - row + NROW) % NCOL


def mirror_owner(row, col):
    shift = lag(row, col)
    return (row + shift + NCOL * (shift == 0).astype(jnp.int32)) % NROW, row % NCOL


def group_kernel(
    start_ref, order_ref, below_ref, cnt_ref, w_ref, dens_hbm, phi_hbm, near_ref, wide_ref, mirrored_ref,
    dens_ref, phi_ref, scaled_ref, phit_ref, sub_ref, stage_ref, back_ref, rho_ref, pot_ref,
    main0_ref, main1_ref, far0_ref, far1_ref, run_ref, turned_ref, relay_ref, keep_ref,
    dens_sem, phi_sem, dsend, drecv, msend, mrecv, fsend, frecv, self_sem, send1, recv1, send2, recv2,
):
    row, col = lax.axis_index("row"), lax.axis_index("col")
    me = row * NCOL + col

    def column(k):
        return pl.ds(k * B, B)

    dens_copies = [
        pltpu.make_async_copy(dens_hbm.at[:, :, column(k)], dens_ref.at[k], dens_sem) for k in range(ENTRIES)
    ]
    for copy in dens_copies:
        copy.start()

    def load_phi(half):
        for k in range(ENTRIES):
            pltpu.make_async_copy(
                phi_hbm.at[pl.ds(half * (ROWS // 2), ROWS // 2), column(k)], phi_ref.at[k], phi_sem
            ).start()

    load_phi(0)

    barrier = pltpu.get_barrier_semaphore()

    def greet(i, carry):
        r, c = offset_target(i, row, col)
        pl.semaphore_signal(barrier, inc=1, device_id=(r, c), device_id_type=MESH)
        return carry

    lax.fori_loop(1, GROUPS, greet, 0)

    def pick(r, c):
        start = start_ref[r * NCOL + c]
        i = position(start, row) >> 4
        j0 = position(start, col) >> 3
        j1 = position(start, col + NCOL) >> 3
        return dens_ref[j0, i], dens_ref[j1, i]

    pltpu.make_async_copy(dens_ref, dens_ref, dens_sem).wait()

    def staged(n, r, c):
        at = (n * GROUPS + r * NCOL + c) * GATHER_ROWS
        return pl.ds(pl.multiple_of(at, GATHER_ROWS), GATHER_ROWS)

    def prepare(i, carry):
        r, c = offset_target(i, row, col)
        left, right = pick(r, c)
        for n in range(GATHER_ROUNDS):
            part = slice(n * GATHER_ROWS, (n + 1) * GATHER_ROWS)
            stage_ref[staged(n, r, c), pl.ds(0, B)] = left[part]
            stage_ref[staged(n, r, c), pl.ds(B, B)] = right[part]
        return carry

    lax.fori_loop(1, GROUPS, prepare, 0)
    my_rows = pl.ds(pl.multiple_of(place(row) * GATHER_ROWS, GATHER_ROWS), GATHER_ROWS)
    my_cols = pl.ds(pl.multiple_of(col * 2 * B, B), 2 * B)
    left, right = pick(row, col)
    for n in range(GATHER_ROUNDS):
        part = slice(n * GATHER_ROWS, (n + 1) * GATHER_ROWS)
        sub_ref[n, my_rows, my_cols] = jnp.concatenate([left[part], right[part]], axis=1)

    pl.semaphore_wait(barrier, GROUPS - 1)

    def send_round(n, carry):
        def send(i, carry):
            r, c = offset_target(i, row, col)
            pltpu.make_async_remote_copy(
                src_ref=stage_ref.at[staged(n, r, c)],
                dst_ref=sub_ref.at[n, my_rows, my_cols],
                send_sem=dsend, recv_sem=drecv.at[n],
                device_id=(r, c), device_id_type=MESH,
            ).start()
            return carry

        return lax.fori_loop(1, GROUPS, send, carry)

    lax.fori_loop(0, GATHER_ROUNDS, send_round, 0)

    my_start = start_ref[me]
    my_count = cnt_ref[me]

    for half in range(2):
        pltpu.make_async_copy(phi_ref, phi_ref, phi_sem).wait()

        def turn(at, carry):
            residue = at // 2 + (at % 2) * NCOL
            k = list_place(my_start, residue)
            live = jnp.clip(my_count - k, 0, 1).astype(jnp.float32)
            for t in range(ROWS // 2 // B):
                tile = phi_ref[k, pl.ds(t * B, B), :]
                tile = (tile.astype(jnp.float32) * live).T
                phit_ref[at, :, pl.ds(half * (ROWS // 2) + t * B, B)] = tile.astype(jnp.bfloat16)
            return carry

        lax.fori_loop(0, ENTRIES, turn, 0)
        if half == 0:
            load_phi(1)

    shift = lag(row, col)

    def segment(start, apart):
        k = list_place(start, row)
        whole = jnp.clip(ENTRIES - apart - k, 0, 1)
        return ((start + k) >> 4) * 2 + whole

    def keeps(m, carry):
        for at, apart in ((0, shift), (1, NCOL)):
            same = 1 - jnp.clip(segment(start_ref[order_ref[m]], apart) - segment(start_ref[order_ref[m - 1]], apart), 0, 1)
            keep_ref[at, m] = same.astype(jnp.float32)
        return carry

    keep_ref[0, 0] = 0.0
    keep_ref[1, 0] = 0.0
    lax.fori_loop(1, GROUPS, keeps, 0)
    rho_ref[...] = jnp.zeros_like(rho_ref)

    M, N = ENTRIES * GATHER_ROWS, 256
    one_round = stage_ref.at[pl.ds(0, (GROUPS - 1) * GATHER_ROWS)]

    def density_round(n, carry):
        pltpu.make_async_copy(one_round, one_round, drecv.at[n]).wait()
        rows = pl.ds(pl.multiple_of(n * GATHER_ROWS, GATHER_ROWS), GATHER_ROWS)

        def density(step, carry):
            cols = pl.ds(pl.multiple_of(step * N, N), N)
            g = jnp.dot(
                sub_ref[n], phit_ref[:, :, cols].reshape(WIDTH, N), preferred_element_type=jnp.float32
            )
            g = g * phit_ref[:, rows, cols].reshape(M, N).astype(jnp.float32)
            rho_ref[:, cols] += jnp.sum(g.reshape(M // 8, 8, N), axis=0)
            return carry

        return lax.fori_loop(0, ROWS // N, density, carry)

    lax.fori_loop(0, GATHER_ROUNDS, density_round, 0)

    rho = jnp.sum(rho_ref[...], axis=0, keepdims=True)
    pot_ref[...] = w_ref[...] * rho * jnp.exp(jnp.log(1.0 + rho * rho) * (-1.0 / 3.0))

    def weigh(c, carry):
        scaled_ref[c] = (
            phit_ref[pl.ds(c * 2, 2)].reshape(2 * B, ROWS).astype(jnp.float32) * pot_ref[...]
        ).astype(jnp.bfloat16)
        return carry

    lax.fori_loop(0, NCOL, weigh, 0)

    HALF = ENTRIES // 2
    main_refs, far_refs = (main0_ref, main1_ref), (far0_ref, far1_ref)

    def return_round(n):
        rows = pl.ds(pl.multiple_of(n * RETURN_ROWS, RETURN_ROWS), RETURN_ROWS)

        def potential(step, carry):
            c, half = step // 2, step % 2
            v = lax.dot_general(
                phit_ref[pl.ds(half * HALF, HALF), rows, :].reshape(HALF * RETURN_ROWS, ROWS), scaled_ref[c],
                (((1,), (1,)), ((), ())), preferred_element_type=jnp.float32,
            ).astype(jnp.bfloat16).reshape(HALF, RETURN_ROWS, 2 * B)
            back_ref[n, c * 2, pl.ds(half * HALF, HALF)] = v[:, :, :B]
            back_ref[n, c * 2 + 1, pl.ds(half * HALF, HALF)] = v[:, :, B:]
            return carry

        lax.fori_loop(0, NCOL * 2, potential, 0)

        def main_copy(r, c):
            residue = (r + lag(r, c)) % NROW
            return pltpu.make_async_remote_copy(
                src_ref=back_ref.at[n, place(residue), place(r)],
                dst_ref=main_refs[n].at[me],
                send_sem=msend, recv_sem=mrecv.at[n],
                device_id=(r, c), device_id_type=MESH,
            )

        def far_copy(r, c):
            residue = (r + NCOL) % NROW
            return pltpu.make_async_remote_copy(
                src_ref=back_ref.at[n, place(residue), place(r)],
                dst_ref=far_refs[n].at[me],
                send_sem=fsend, recv_sem=frecv.at[n],
                device_id=(r, c), device_id_type=MESH,
            )

        def give(i, carry):
            r, c = offset_target(i, row, col)
            main_copy(r, c).start()

            @pl.when(lag(r, c) == 0)
            def _():
                far_copy(r, c).start()

            return carry

        lax.fori_loop(1, GROUPS, give, 0)
        residue = (row + lag(row, col)) % NROW
        own = pltpu.make_async_copy(back_ref.at[n, place(residue), place(row)], main_refs[n].at[me], self_sem)
        own.start()
        own.wait()

        @pl.when(lag(row, col) == 0)
        def _():
            residue = (row + NCOL) % NROW
            own = pltpu.make_async_copy(back_ref.at[n, place(residue), place(row)], far_refs[n].at[me], self_sem)
            own.start()
            own.wait()

    for n in range(RETURN_ROUNDS):
        return_round(n)
    gathered = stage_ref.at[pl.ds(0, (GROUPS - 1) * B)]
    pltpu.make_async_copy(gathered, gathered, dsend).wait()

    def relay_shift(i):
        return (5 * i + 1) % NROW, (3 * i) % NCOL

    def relay(i):
        dr, dc = relay_shift(i)
        return (row + dr) % NROW, (col + dc) % NCOL

    def final(i):
        dr, dc = relay_shift(i)
        return mirror_owner((row - dr + NROW) % NROW, (col - dc + NCOL) % NCOL)

    def first(n, i):
        return pltpu.make_async_remote_copy(
            src_ref=turned_ref.at[n, i], dst_ref=relay_ref.at[n, i], send_sem=send1.at[n, i], recv_sem=recv1.at[n, i],
            device_id=relay(i), device_id_type=MESH,
        )

    def second(n, i):
        return pltpu.make_async_remote_copy(
            src_ref=relay_ref.at[n, i], dst_ref=mirrored_ref.at[n, i], send_sem=send2.at[n, i], recv_sem=recv2.at[n, i],
            device_id=final(i), device_id_type=MESH,
        )

    def stays(i):
        r, c = final(i)
        return r * NCOL + c == me

    def total(parts_ref, n, which, apart, out_ref):
        for u in range(RETURN_ROWS // RUN):
            rows = pl.ds(u * RUN, RUN)

            def add(m, acc):
                acc = acc * keep_ref[which, m] + parts_ref[order_ref[m], rows, :].astype(jnp.float32)
                run_ref[m] = acc
                return acc

            lax.fori_loop(0, GROUPS, add, jnp.zeros((RUN, B), jnp.float32))
            out_rows = pl.ds(pl.multiple_of(n * RETURN_ROWS + u * RUN, RUN), RUN)

            def slot(at, carry):
                i, w = at // 2, at % 2

                def ended(i):
                    p = row + i * NROW
                    low = jnp.where(w == 1, p - 15, p - 15 + apart)
                    high = jnp.where(w == 1, p - 15 + apart, p + 1)
                    before = below_ref[jnp.clip(low, 0, GROUPS)]
                    until = below_ref[jnp.clip(high, 0, GROUPS)]
                    some = jnp.clip(until - before, 0, 1).astype(jnp.float32)
                    return run_ref[jnp.maximum(until - 1, 0)] * some

                out_ref[at, out_rows, :] = ended(i)

                @pl.when(i == 0)
                def _():
                    out_ref[at, out_rows, :] += ended(BLOCK_ROWS)

                return carry

            lax.fori_loop(0, SLOTS, slot, 0)

    one_part = stage_ref.at[pl.ds(0, (GROUPS - 1) * RETURN_ROWS // 2)]

    def finish_round(n):
        pltpu.make_async_copy(one_part, one_part, mrecv.at[n]).wait()
        total(main_refs[n], n, 0, shift, near_ref)

        def start_first(i, carry):
            rows = pl.ds(pl.multiple_of(n * RETURN_ROWS, RETURN_ROWS), RETURN_ROWS)
            turned_ref[n, i] = near_ref[i, rows, :].astype(jnp.bfloat16)
            first(n, i).start()
            return carry

        lax.fori_loop(0, SLOTS, start_first, 0)

        @pl.when(shift == 0)
        def _():
            pltpu.make_async_copy(one_part, one_part, frecv.at[n]).wait()
            total(far_refs[n], n, 1, NCOL, wide_ref)

        def pass_on(i, carry):
            first(n, i).wait_recv()

            @pl.when(jnp.logical_not(stays(i)))
            def _():
                second(n, i).start()

            @pl.when(stays(i))
            def _():
                pltpu.make_async_copy(relay_ref.at[n, i], mirrored_ref.at[n, i], recv2.at[n, i]).start()

            return carry

        lax.fori_loop(0, SLOTS, pass_on, 0)

    @pl.when(shift != 0)
    def _():
        wide_ref[...] = jnp.zeros_like(wide_ref)

    for n in range(RETURN_ROUNDS):
        finish_round(n)

    def done(at, carry):
        n, i = at // SLOTS, at % SLOTS
        first(n, i).wait_send()
        second(n, i).wait_recv()

        @pl.when(jnp.logical_not(stays(i)))
        def _():
            second(n, i).wait_send()

        return carry

    lax.fori_loop(0, RETURN_ROUNDS * SLOTS, done, 0)

    sent = stage_ref.at[pl.ds(0, (GROUPS - 1) * B // 2)]
    pltpu.make_async_copy(sent, sent, msend).wait()

    @pl.when(shift == 0)
    def _():
        others = stage_ref.at[pl.ds(0, (NROW - 1) * B // 2)]
        pltpu.make_async_copy(others, others, fsend).wait()

    @pl.when(shift != 0)
    def _():
        others = stage_ref.at[pl.ds(0, NROW * B // 2)]
        pltpu.make_async_copy(others, others, fsend).wait()


VMEM = pl.BlockSpec(memory_space=pltpu.VMEM)
SMEM = pl.BlockSpec(memory_space=pltpu.SMEM)
HBM = pl.BlockSpec(memory_space=pl.ANY)


def exchange(starts, order, below, cnt, w, dens, phi):
    sums = jax.ShapeDtypeStruct((SLOTS, B, B), jnp.float32)
    parts = (GROUPS, RETURN_ROWS, B)
    slots = (RETURN_ROUNDS, SLOTS, RETURN_ROWS, B)
    dma = pltpu.SemaphoreType.DMA
    return pl.pallas_call(
        group_kernel,
        out_shape=[sums, sums, jax.ShapeDtypeStruct(slots, jnp.bfloat16)],
        in_specs=[SMEM, SMEM, SMEM, SMEM, VMEM, HBM, HBM],
        out_specs=[VMEM, VMEM, VMEM],
        scratch_shapes=[
            pltpu.VMEM((ENTRIES, BLOCK_ROWS, B, B), jnp.bfloat16),
            pltpu.VMEM((ENTRIES, ROWS // 2, B), jnp.bfloat16),
            pltpu.VMEM((NCOL, 2 * B, ROWS), jnp.bfloat16),
            pltpu.VMEM((ENTRIES, B, ROWS), jnp.bfloat16),
            pltpu.VMEM((GATHER_ROUNDS, ENTRIES * GATHER_ROWS, WIDTH), jnp.bfloat16),
            pltpu.VMEM((GROUPS * B, 2 * B), jnp.bfloat16),
            pltpu.VMEM((RETURN_ROUNDS, ENTRIES, ENTRIES, RETURN_ROWS, B), jnp.bfloat16),
            pltpu.VMEM((8, ROWS), jnp.float32),
            pltpu.VMEM((1, ROWS), jnp.float32),
            pltpu.VMEM(parts, jnp.bfloat16),
            pltpu.VMEM(parts, jnp.bfloat16),
            pltpu.VMEM(parts, jnp.bfloat16),
            pltpu.VMEM(parts, jnp.bfloat16),
            pltpu.VMEM((GROUPS, RUN, B), jnp.float32),
            pltpu.VMEM(slots, jnp.bfloat16),
            pltpu.VMEM(slots, jnp.bfloat16),
            pltpu.SMEM((2, GROUPS), jnp.float32),
            dma, dma, dma, dma((GATHER_ROUNDS,)), dma, dma((RETURN_ROUNDS,)), dma, dma((RETURN_ROUNDS,)), dma,
        ] + [dma((RETURN_ROUNDS, SLOTS))] * 4,
        compiler_params=pltpu.CompilerParams(
            collective_id=0, has_side_effects=True, vmem_limit_bytes=61 << 20
        ),
        cost_estimate=pl.CostEstimate(flops=4 * ROWS * WIDTH * WIDTH, bytes_accessed=16 << 20, transcendentals=2 * ROWS),
    )(starts, order, below, cnt, w, dens, phi)


def sort_kernel(list_ref, home_ref, start_ref, order_ref, below_ref, next_ref):
    def clear(v, carry):
        below_ref[v] = 0
        return carry

    def count(g, carry):
        start = home_ref[list_ref[g, 0]]
        start_ref[g] = start
        below_ref[start + 1] += 1
        return carry

    def add(v, before):
        before = before + below_ref[v]
        below_ref[v] = before
        next_ref[v] = before
        return before

    def put(g, carry):
        start = start_ref[g]
        at = next_ref[start]
        order_ref[at] = g
        next_ref[start] = at + 1
        return carry

    lax.fori_loop(0, GROUPS + 8, clear, 0, unroll=8)
    lax.fori_loop(0, GROUPS, count, 0, unroll=8)
    lax.fori_loop(0, GROUPS + 8, add, 0, unroll=8)
    lax.fori_loop(0, GROUPS, put, 0, unroll=8)


def sort_starts(lists, home):
    return pl.pallas_call(
        sort_kernel,
        out_shape=[
            jax.ShapeDtypeStruct((GROUPS,), jnp.int32),
            jax.ShapeDtypeStruct((GROUPS,), jnp.int32),
            jax.ShapeDtypeStruct((GROUPS + 8,), jnp.int32),
        ],
        in_specs=[SMEM, SMEM],
        out_specs=[SMEM, SMEM, SMEM],
        scratch_shapes=[pltpu.SMEM((GROUPS + 8,), jnp.int32)],
    )(lists, home)


def place_kernel(where_ref, near_ref, wide_ref, mirrored_ref, out_ref):
    row, col = where_ref[0], where_ref[1]
    i = pl.program_id(0)
    shift = lag(row, col)
    out_ref[...] = jnp.zeros_like(out_ref)
    p = row + NROW * i

    def columns(q):
        return pl.ds(pl.multiple_of(((q & (GROUPS - 1)) >> 3) * B, B), B)

    @pl.when(shift == 0)
    def _():
        out_ref[:, columns(p)] = near_ref[i * 2]
        for w in range(2):
            out_ref[:, columns(p + NCOL - NROW * w)] = wide_ref[i * 2 + w]

    @pl.when(shift != 0)
    def _():
        for w in range(2):
            out_ref[:, columns(p + shift - NROW * w)] = near_ref[i * 2 + w]
            there = p - (NCOL - shift) + NROW * w
            at = ((there & (GROUPS - 1)) >> 4) * 2 + w
            block = jnp.concatenate([mirrored_ref[n, at] for n in range(RETURN_ROUNDS)], axis=0)
            out_ref[:, columns(there)] = block.astype(jnp.float32).T


def assemble(where, near, wide, mirrored):
    return pl.pallas_call(
        place_kernel,
        grid=(BLOCK_ROWS,),
        out_shape=jax.ShapeDtypeStruct((BLOCK_ROWS * B, WIDTH), jnp.float32),
        in_specs=[SMEM, VMEM, VMEM, VMEM],
        out_specs=pl.BlockSpec((B, WIDTH), lambda i: (i, 0)),
    )(where, near, wide, mirrored)


def body(basis_values, point_weights, density_stored, relevant_blocks, relevant_count, block_home):
    starts, order, below = sort_starts(relevant_blocks, block_home)
    near, wide, mirrored = exchange(
        starts, order, below, relevant_count, point_weights.reshape(1, ROWS),
        density_stored.reshape(BLOCK_ROWS, B, WIDTH), basis_values,
    )
    where = jnp.stack([lax.axis_index("row"), lax.axis_index("col")]).astype(jnp.int32)
    return assemble(where, near, wide, mirrored)


def solution(mesh):
    in_specs = (P(("row", "col"), None), P(("row", "col")), P("row", "col"), P(), P(), P())
    return jax.shard_map(body, mesh=mesh, in_specs=in_specs, out_specs=P("row", "col"), check_vma=False)
```

```python
import jax
import jax.numpy as jnp
from jax import lax
from jax.experimental import pallas as pl
from jax.experimental.pallas import tpu as pltpu
from jax.sharding import PartitionSpec as P

MESH = pl.DeviceIdType.MESH
NROW, NCOL, GROUPS, B = 16, 8, 128, 128
ENTRIES = 16
ROWS = 1536
WIDTH = ENTRIES * B
BLOCK_ROWS = 8
GATHER_ROUNDS, GATHER_ROWS = 4, 32
RETURN_ROUNDS, RETURN_ROWS = 2, 64
RUN = 32
SLOTS = 2 * BLOCK_ROWS


def place(residue):
    return (residue % NCOL) * 2 + residue // NCOL


def offset_target(step, row, col):
    t = (step * (step + 1) // 2) % GROUPS
    y = (row // 4 + t % 4) % 4
    x = (row % 4 + (t // 4) % 4) % 4
    z = (col // 2 + (t // 16) % 4) % 4
    core = (col + t // 64) % 2
    return y * 4 + x, z * 2 + core


def list_place(start, residue):
    return (residue - start) & (ENTRIES - 1)


def position(start, residue):
    return (start + list_place(start, residue)) & (GROUPS - 1)


def lag(row, col):
    return (col - row + NROW) % NCOL


def mirror_owner(row, col):
    shift = lag(row, col)
    return (row + shift + NCOL * (shift == 0).astype(jnp.int32)) % NROW, row % NCOL


def group_kernel(
    first_ref, home_ref, first_row, home_row, cnt_ref, w_ref, dens_hbm, phi_hbm, near_ref, wide_ref, mirrored_ref,
    dens_ref, phi_ref, scaled_ref, phit_ref, sub_ref, stage_ref, back_ref, rho_ref, pot_ref,
    main_refs, far_refs, run_ref, turned_ref, relay_ref, keep_ref, table_ref, order_ref,
    table_sem, dens_sem, phi_sem, dsend, drecv, msend, mrecv, fsend, frecv, self_sem, send1, recv1, send2, recv2,
):
    row, col = lax.axis_index("row"), lax.axis_index("col")
    me = row * NCOL + col

    def start_of(group):
        return home_ref[first_ref[0, group]]

    def column(k):
        return pl.ds(k * B, B)

    dens_copies = [
        pltpu.make_async_copy(dens_hbm.at[:, :, column(k)], dens_ref.at[k], dens_sem) for k in range(ENTRIES)
    ]
    for copy in dens_copies:
        copy.start()

    def load_phi(half):
        for k in range(ENTRIES):
            pltpu.make_async_copy(
                phi_hbm.at[pl.ds(half * (ROWS // 2), ROWS // 2), column(k)], phi_ref.at[k], phi_sem
            ).start()

    load_phi(0)

    barrier = pltpu.get_barrier_semaphore()

    def greet(i, carry):
        r, c = offset_target(i, row, col)
        pl.semaphore_signal(barrier, inc=1, device_id=(r, c), device_id_type=MESH)
        return carry

    lax.fori_loop(1, GROUPS, greet, 0)

    def pick(r, c):
        start = start_of(r * NCOL + c)
        i = position(start, row) >> 4
        j0 = position(start, col) >> 3
        j1 = position(start, col + NCOL) >> 3
        return dens_ref[j0, i], dens_ref[j1, i]

    pltpu.make_async_copy(dens_ref, dens_ref, dens_sem).wait()

    def staged(n, r, c):
        at = (n * GROUPS + r * NCOL + c) * GATHER_ROWS
        return pl.ds(pl.multiple_of(at, GATHER_ROWS), GATHER_ROWS)

    def prepare(i, carry):
        r, c = offset_target(i, row, col)
        left, right = pick(r, c)
        for n in range(GATHER_ROUNDS):
            part = slice(n * GATHER_ROWS, (n + 1) * GATHER_ROWS)
            stage_ref[staged(n, r, c), pl.ds(0, B)] = left[part]
            stage_ref[staged(n, r, c), pl.ds(B, B)] = right[part]
        return carry

    lax.fori_loop(1, GROUPS, prepare, 0)
    my_rows = pl.ds(pl.multiple_of(place(row) * GATHER_ROWS, GATHER_ROWS), GATHER_ROWS)
    my_cols = pl.ds(pl.multiple_of(col * 2 * B, B), 2 * B)
    left, right = pick(row, col)
    for n in range(GATHER_ROUNDS):
        part = slice(n * GATHER_ROWS, (n + 1) * GATHER_ROWS)
        sub_ref[n, my_rows, my_cols] = jnp.concatenate([left[part], right[part]], axis=1)

    pl.semaphore_wait(barrier, GROUPS - 1)

    def send_round(n, carry):
        def send(i, carry):
            r, c = offset_target(i, row, col)
            pltpu.make_async_remote_copy(
                src_ref=stage_ref.at[staged(n, r, c)],
                dst_ref=sub_ref.at[n, my_rows, my_cols],
                send_sem=dsend, recv_sem=drecv.at[n],
                device_id=(r, c), device_id_type=MESH,
            ).start()
            return carry

        return lax.fori_loop(1, GROUPS, send, carry)

    lax.fori_loop(0, GATHER_ROUNDS, send_round, 0)

    my_start = start_of(me)
    my_count = cnt_ref[me]

    for half in range(2):
        pltpu.make_async_copy(phi_ref, phi_ref, phi_sem).wait()

        def turn(at, carry):
            residue = at // 2 + (at % 2) * NCOL
            k = list_place(my_start, residue)
            live = jnp.clip(my_count - k, 0, 1).astype(jnp.float32)
            for t in range(ROWS // 2 // B):
                tile = phi_ref[k, pl.ds(t * B, B), :]
                tile = (tile.astype(jnp.float32) * live).T
                phit_ref[at, :, pl.ds(half * (ROWS // 2) + t * B, B)] = tile.astype(jnp.bfloat16)
            return carry

        lax.fori_loop(0, ENTRIES, turn, 0)
        if half == 0:
            load_phi(1)

    shift = lag(row, col)

    lane = lax.broadcasted_iota(jnp.int32, (GROUPS, GROUPS), 1)
    line = lax.broadcasted_iota(jnp.int32, (GROUPS, GROUPS), 0)
    homes = jnp.broadcast_to(home_row[...], (GROUPS, GROUPS)).T
    starts = jnp.sum(jnp.where(first_row[0:1, :] == line, homes, 0), axis=0, keepdims=True)
    across = jnp.broadcast_to(starts, (GROUPS, GROUPS))
    down = across.T
    ahead = ((across < down) | ((across == down) & (lane < line))).astype(jnp.int32)
    rank = jnp.sum(ahead, axis=1, keepdims=True)
    table_ref[0:1, :] = jnp.sum(jnp.where(rank == lane, line, 0), axis=0, keepdims=True)
    table_ref[1:2, :] = jnp.sum((down < lane).astype(jnp.int32), axis=0, keepdims=True)
    table_ref[2:3, :] = jnp.sum((down < lane + GROUPS).astype(jnp.int32), axis=0, keepdims=True)
    table_ref[3:4, :] = jnp.sum(jnp.where(rank == lane, down, 0), axis=0, keepdims=True)
    tables = pltpu.make_async_copy(table_ref, order_ref, table_sem)
    tables.start()
    tables.wait()

    def below(at):
        return order_ref[1 + at // GROUPS, at % GROUPS]

    def segment(start, apart):
        k = list_place(start, row)
        whole = jnp.clip(ENTRIES - apart - k, 0, 1)
        return ((start + k) >> 4) * 2 + whole

    def keeps(m, carry):
        for at, apart in ((0, shift), (1, NCOL)):
            same = 1 - jnp.clip(segment(order_ref[3, m], apart) - segment(order_ref[3, m - 1], apart), 0, 1)
            keep_ref[at, m] = same.astype(jnp.float32)
        return carry

    keep_ref[0, 0] = 0.0
    keep_ref[1, 0] = 0.0
    lax.fori_loop(1, GROUPS, keeps, 0)
    rho_ref[...] = jnp.zeros_like(rho_ref)

    M, N = ENTRIES * GATHER_ROWS, 256
    one_round = stage_ref.at[pl.ds(0, (GROUPS - 1) * GATHER_ROWS)]

    def density_round(n, carry):
        pltpu.make_async_copy(one_round, one_round, drecv.at[n]).wait()
        rows = pl.ds(pl.multiple_of(n * GATHER_ROWS, GATHER_ROWS), GATHER_ROWS)

        def density(step, carry):
            cols = pl.ds(pl.multiple_of(step * N, N), N)
            g = jnp.dot(
                sub_ref[n], phit_ref[:, :, cols].reshape(WIDTH, N), preferred_element_type=jnp.float32
            )
            g = g * phit_ref[:, rows, cols].reshape(M, N).astype(jnp.float32)
            rho_ref[:, cols] += jnp.sum(g.reshape(M // 8, 8, N), axis=0)
            return carry

        return lax.fori_loop(0, ROWS // N, density, carry)

    lax.fori_loop(0, GATHER_ROUNDS, density_round, 0)

    rho = jnp.sum(rho_ref[...], axis=0, keepdims=True)
    pot_ref[...] = w_ref[...].reshape(1, ROWS) * rho * jnp.exp(jnp.log(1.0 + rho * rho) * (-1.0 / 3.0))

    def weigh(c, carry):
        scaled_ref[c] = (
            phit_ref[pl.ds(c * 2, 2)].reshape(2 * B, ROWS).astype(jnp.float32) * pot_ref[...]
        ).astype(jnp.bfloat16)
        return carry

    lax.fori_loop(0, NCOL, weigh, 0)

    HALF = ENTRIES // 2

    def return_round(n):
        rows = pl.ds(pl.multiple_of(n * RETURN_ROWS, RETURN_ROWS), RETURN_ROWS)

        def potential(step, carry):
            c, half = step // 2, step % 2
            v = lax.dot_general(
                phit_ref[pl.ds(half * HALF, HALF), rows, :].reshape(HALF * RETURN_ROWS, ROWS), scaled_ref[c],
                (((1,), (1,)), ((), ())), preferred_element_type=jnp.float32,
            ).astype(jnp.bfloat16).reshape(HALF, RETURN_ROWS, 2 * B)
            back_ref[n, c * 2, pl.ds(half * HALF, HALF)] = v[:, :, :B]
            back_ref[n, c * 2 + 1, pl.ds(half * HALF, HALF)] = v[:, :, B:]
            return carry

        lax.fori_loop(0, NCOL * 2, potential, 0)

        def main_copy(r, c):
            residue = (r + lag(r, c)) % NROW
            return pltpu.make_async_remote_copy(
                src_ref=back_ref.at[n, place(residue), place(r)],
                dst_ref=main_refs[n].at[me],
                send_sem=msend, recv_sem=mrecv.at[n],
                device_id=(r, c), device_id_type=MESH,
            )

        def far_copy(r, c):
            residue = (r + NCOL) % NROW
            return pltpu.make_async_remote_copy(
                src_ref=back_ref.at[n, place(residue), place(r)],
                dst_ref=far_refs[n].at[me],
                send_sem=fsend, recv_sem=frecv.at[n],
                device_id=(r, c), device_id_type=MESH,
            )

        def give(i, carry):
            r, c = offset_target(i, row, col)
            main_copy(r, c).start()

            @pl.when(lag(r, c) == 0)
            def _():
                far_copy(r, c).start()

            return carry

        lax.fori_loop(1, GROUPS, give, 0)
        residue = (row + lag(row, col)) % NROW
        own = pltpu.make_async_copy(back_ref.at[n, place(residue), place(row)], main_refs[n].at[me], self_sem)
        own.start()
        own.wait()

        @pl.when(lag(row, col) == 0)
        def _():
            residue = (row + NCOL) % NROW
            own = pltpu.make_async_copy(back_ref.at[n, place(residue), place(row)], far_refs[n].at[me], self_sem)
            own.start()
            own.wait()

    for n in range(RETURN_ROUNDS):
        return_round(n)
    gathered = stage_ref.at[pl.ds(0, (GROUPS - 1) * B)]
    pltpu.make_async_copy(gathered, gathered, dsend).wait()

    def relay_shift(i):
        return (5 * i + 1) % NROW, (3 * i) % NCOL

    def relay(i):
        dr, dc = relay_shift(i)
        return (row + dr) % NROW, (col + dc) % NCOL

    def final(i):
        dr, dc = relay_shift(i)
        return mirror_owner((row - dr + NROW) % NROW, (col - dc + NCOL) % NCOL)

    def first(n, i):
        return pltpu.make_async_remote_copy(
            src_ref=turned_ref.at[n, i], dst_ref=relay_ref.at[n, i], send_sem=send1.at[n, i], recv_sem=recv1.at[n, i],
            device_id=relay(i), device_id_type=MESH,
        )

    def second(n, i):
        return pltpu.make_async_remote_copy(
            src_ref=relay_ref.at[n, i], dst_ref=mirrored_ref.at[n, i], send_sem=send2.at[n, i], recv_sem=recv2.at[n, i],
            device_id=final(i), device_id_type=MESH,
        )

    def stays(i):
        r, c = final(i)
        return r * NCOL + c == me

    def total(parts_ref, n, which, apart, out_ref):
        for u in range(RETURN_ROWS // RUN):
            rows = pl.ds(u * RUN, RUN)

            def add(m, acc):
                acc = acc * keep_ref[which, m] + parts_ref[order_ref[0, m], rows, :].astype(jnp.float32)
                run_ref[m] = acc
                return acc

            lax.fori_loop(0, GROUPS, add, jnp.zeros((RUN, B), jnp.float32))
            out_rows = pl.ds(pl.multiple_of(n * RETURN_ROWS + u * RUN, RUN), RUN)

            def slot(at, carry):
                i, w = at // 2, at % 2

                def ended(i):
                    p = row + i * NROW
                    low = jnp.where(w == 1, p - 15, p - 15 + apart)
                    high = jnp.where(w == 1, p - 15 + apart, p + 1)
                    before = below(jnp.clip(low, 0, GROUPS))
                    until = below(jnp.clip(high, 0, GROUPS))
                    some = jnp.clip(until - before, 0, 1).astype(jnp.float32)
                    return run_ref[jnp.maximum(until - 1, 0)] * some

                out_ref[at, out_rows, :] = ended(i)

                @pl.when(i == 0)
                def _():
                    out_ref[at, out_rows, :] += ended(BLOCK_ROWS)

                return carry

            lax.fori_loop(0, SLOTS, slot, 0)

    one_part = stage_ref.at[pl.ds(0, (GROUPS - 1) * RETURN_ROWS // 2)]

    def finish_round(n):
        pltpu.make_async_copy(one_part, one_part, mrecv.at[n]).wait()
        total(main_refs[n], n, 0, shift, near_ref)

        def start_first(i, carry):
            rows = pl.ds(pl.multiple_of(n * RETURN_ROWS, RETURN_ROWS), RETURN_ROWS)
            turned_ref[n, i] = near_ref[i, rows, :].astype(jnp.bfloat16)
            first(n, i).start()
            return carry

        lax.fori_loop(0, SLOTS, start_first, 0)

        @pl.when(shift == 0)
        def _():
            pltpu.make_async_copy(one_part, one_part, frecv.at[n]).wait()
            total(far_refs[n], n, 1, NCOL, wide_ref)

        def pass_on(i, carry):
            first(n, i).wait_recv()

            @pl.when(jnp.logical_not(stays(i)))
            def _():
                second(n, i).start()

            @pl.when(stays(i))
            def _():
                pltpu.make_async_copy(relay_ref.at[n, i], mirrored_ref.at[n, i], recv2.at[n, i]).start()

            return carry

        lax.fori_loop(0, SLOTS, pass_on, 0)

    @pl.when(shift != 0)
    def _():
        wide_ref[...] = jnp.zeros_like(wide_ref)

    for n in range(RETURN_ROUNDS):
        finish_round(n)

    def done(at, carry):
        n, i = at // SLOTS, at % SLOTS
        first(n, i).wait_send()
        second(n, i).wait_recv()

        @pl.when(jnp.logical_not(stays(i)))
        def _():
            second(n, i).wait_send()

        return carry

    lax.fori_loop(0, RETURN_ROUNDS * SLOTS, done, 0)

    sent = stage_ref.at[pl.ds(0, (GROUPS - 1) * B // 2)]
    pltpu.make_async_copy(sent, sent, msend).wait()

    @pl.when(shift == 0)
    def _():
        others = stage_ref.at[pl.ds(0, (NROW - 1) * B // 2)]
        pltpu.make_async_copy(others, others, fsend).wait()

    @pl.when(shift != 0)
    def _():
        others = stage_ref.at[pl.ds(0, NROW * B // 2)]
        pltpu.make_async_copy(others, others, fsend).wait()


VMEM = pl.BlockSpec(memory_space=pltpu.VMEM)
SMEM = pl.BlockSpec(memory_space=pltpu.SMEM)
HBM = pl.BlockSpec(memory_space=pl.ANY)


def exchange(lists, home, cnt, w, dens, phi):
    sums = jax.ShapeDtypeStruct((SLOTS, B, B), jnp.float32)
    parts = (GROUPS, RETURN_ROWS, B)
    slots = (RETURN_ROUNDS, SLOTS, RETURN_ROWS, B)
    dma = pltpu.SemaphoreType.DMA
    return pl.pallas_call(
        group_kernel,
        out_shape=[sums, sums, jax.ShapeDtypeStruct(slots, jnp.bfloat16)],
        in_specs=[SMEM, SMEM, VMEM, VMEM, SMEM, VMEM, HBM, HBM],
        out_specs=[VMEM, VMEM, VMEM],
        scratch_shapes=[
            pltpu.VMEM((ENTRIES, BLOCK_ROWS, B, B), jnp.bfloat16),
            pltpu.VMEM((ENTRIES, ROWS // 2, B), jnp.bfloat16),
            pltpu.VMEM((NCOL, 2 * B, ROWS), jnp.bfloat16),
            pltpu.VMEM((ENTRIES, B, ROWS), jnp.bfloat16),
            pltpu.VMEM((GATHER_ROUNDS, ENTRIES * GATHER_ROWS, WIDTH), jnp.bfloat16),
            pltpu.VMEM((GROUPS * B, 2 * B), jnp.bfloat16),
            pltpu.VMEM((RETURN_ROUNDS, ENTRIES, ENTRIES, RETURN_ROWS, B), jnp.bfloat16),
            pltpu.VMEM((8, ROWS), jnp.float32),
            pltpu.VMEM((1, ROWS), jnp.float32),
            [pltpu.VMEM(parts, jnp.bfloat16)] * RETURN_ROUNDS,
            [pltpu.VMEM(parts, jnp.bfloat16)] * RETURN_ROUNDS,
            pltpu.VMEM((GROUPS, RUN, B), jnp.float32),
            pltpu.VMEM(slots, jnp.bfloat16),
            pltpu.VMEM(slots, jnp.bfloat16),
            pltpu.SMEM((2, GROUPS), jnp.float32),
            pltpu.VMEM((8, GROUPS), jnp.int32),
            pltpu.SMEM((8, GROUPS), jnp.int32),
            dma, dma, dma, dma, dma((GATHER_ROUNDS,)), dma, dma((RETURN_ROUNDS,)), dma, dma((RETURN_ROUNDS,)), dma,
        ] + [dma((RETURN_ROUNDS, SLOTS))] * 4,
        compiler_params=pltpu.CompilerParams(
            collective_id=0, has_side_effects=True, vmem_limit_bytes=61 << 20
        ),
        cost_estimate=pl.CostEstimate(flops=4 * ROWS * WIDTH * WIDTH, bytes_accessed=16 << 20, transcendentals=2 * ROWS),
    )(lists, home, lists, home.reshape(1, GROUPS), cnt, w, dens, phi)


def place_kernel(near_ref, wide_ref, mirrored_ref, out_ref):
    row, col = lax.axis_index("row"), lax.axis_index("col")
    i = pl.program_id(0)
    shift = lag(row, col)
    out_ref[...] = jnp.zeros_like(out_ref)
    p = row + NROW * i

    def columns(q):
        return pl.ds(pl.multiple_of(((q & (GROUPS - 1)) >> 3) * B, B), B)

    @pl.when(shift == 0)
    def _():
        out_ref[:, columns(p)] = near_ref[0]
        for w in range(2):
            out_ref[:, columns(p + NCOL - NROW * w)] = wide_ref[w]

    @pl.when(shift != 0)
    def _():
        for w in range(2):
            out_ref[:, columns(p + shift - NROW * w)] = near_ref[w]
            there = p - (NCOL - shift) + NROW * w
            at = ((there & (GROUPS - 1)) >> 4) * 2 + w
            block = jnp.concatenate([mirrored_ref[n, at] for n in range(RETURN_ROUNDS)], axis=0)
            out_ref[:, columns(there)] = block.astype(jnp.float32).T


def assemble(near, wide, mirrored):
    def wide_index(i):
        return i * (lag(lax.axis_index("row"), lax.axis_index("col")) == 0).astype(jnp.int32), 0, 0

    return pl.pallas_call(
        place_kernel,
        grid=(BLOCK_ROWS,),
        out_shape=jax.ShapeDtypeStruct((BLOCK_ROWS * B, WIDTH), jnp.float32),
        in_specs=[
            pl.BlockSpec((2, B, B), lambda i: (i, 0, 0)),
            pl.BlockSpec((2, B, B), wide_index),
            VMEM,
        ],
        out_specs=pl.BlockSpec((B, WIDTH), lambda i: (i, 0)),
    )(near, wide, mirrored)


def body(basis_values, point_weights, density_stored, relevant_blocks, relevant_count, block_home):
    near, wide, mirrored = exchange(
        relevant_blocks.T, block_home, relevant_count, point_weights,
        density_stored.reshape(BLOCK_ROWS, B, WIDTH), basis_values,
    )
    return assemble(near, wide, mirrored)


def solution(mesh):
    in_specs = (P(("row", "col"), None), P(("row", "col")), P("row", "col"), P(), P(), P())
    return jax.shard_map(body, mesh=mesh, in_specs=in_specs, out_specs=P("row", "col"), check_vma=False)
```

```python
import jax
import jax.numpy as jnp
from jax import lax
from jax.experimental import pallas as pl
from jax.experimental.pallas import tpu as pltpu
from jax.sharding import PartitionSpec as P

MESH = pl.DeviceIdType.MESH
NROW, NCOL, GROUPS, B = 16, 8, 128, 128
ENTRIES = 16
ROWS = 1536
WIDTH = ENTRIES * B
BLOCK_ROWS = 8
GATHER_ROUNDS, GATHER_ROWS = 4, 32
RETURN_ROUNDS, RETURN_ROWS = 2, 64
RUN = 32
SLOTS = 2 * BLOCK_ROWS


def place(residue):
    return (residue % NCOL) * 2 + residue // NCOL


def offset_target(step, row, col):
    t = (step * (step + 1) // 2) % GROUPS
    y = (row // 4 + t % 4) % 4
    x = (row % 4 + (t // 4) % 4) % 4
    z = (col // 2 + (t // 16) % 4) % 4
    core = (col + t // 64) % 2
    return y * 4 + x, z * 2 + core


def list_place(start, residue):
    return (residue - start) & (ENTRIES - 1)


def position(start, residue):
    return (start + list_place(start, residue)) & (GROUPS - 1)


def lag(row, col):
    return (col - row + NROW) % NCOL


def keeps_far(row, col):
    return (lag(row, col) == 0) & (row < NCOL)


def mirror_owner(row, col):
    shift = lag(row, col)
    return (row + shift + NCOL * (shift == 0).astype(jnp.int32)) % NROW, row % NCOL


def group_kernel(
    first_ref, home_ref, first_row, home_row, cnt_ref, w_ref, dens_hbm, phi_hbm, near_ref, wide_ref, mirrored_ref,
    dens_ref, phi_ref, scaled_ref, phit_ref, sub_ref, stage_ref, back_ref, rho_ref, pot_ref,
    main_refs, far_refs, run_ref, turned_ref, relay_ref, keep_ref, table_ref, order_ref,
    table_sem, dens_sem, phi_sem, dsend, drecv, msend, mrecv, fsend, frecv, self_sem, send1, recv1, send2, recv2,
):
    row, col = lax.axis_index("row"), lax.axis_index("col")
    me = row * NCOL + col

    def start_of(group):
        return home_ref[first_ref[0, group]]

    def column(k):
        return pl.ds(k * B, B)

    dens_copies = [
        pltpu.make_async_copy(dens_hbm.at[:, :, column(k)], dens_ref.at[k], dens_sem) for k in range(ENTRIES)
    ]
    for copy in dens_copies:
        copy.start()

    def load_phi(half):
        for k in range(ENTRIES):
            pltpu.make_async_copy(
                phi_hbm.at[pl.ds(half * (ROWS // 2), ROWS // 2), column(k)], phi_ref.at[k], phi_sem
            ).start()

    load_phi(0)

    barrier = pltpu.get_barrier_semaphore()

    def greet(i, carry):
        r, c = offset_target(i, row, col)
        pl.semaphore_signal(barrier, inc=1, device_id=(r, c), device_id_type=MESH)
        return carry

    lax.fori_loop(1, GROUPS, greet, 0)

    def pick(r, c):
        start = start_of(r * NCOL + c)
        i = position(start, row) >> 4
        j0 = position(start, col) >> 3
        j1 = position(start, col + NCOL) >> 3
        return dens_ref[j0, i], dens_ref[j1, i]

    pltpu.make_async_copy(dens_ref, dens_ref, dens_sem).wait()

    def staged(n, r, c):
        at = (n * GROUPS + r * NCOL + c) * GATHER_ROWS
        return pl.ds(pl.multiple_of(at, GATHER_ROWS), GATHER_ROWS)

    def prepare(i, carry):
        r, c = offset_target(i, row, col)
        left, right = pick(r, c)
        for n in range(GATHER_ROUNDS):
            part = slice(n * GATHER_ROWS, (n + 1) * GATHER_ROWS)
            stage_ref[staged(n, r, c), pl.ds(0, B)] = left[part]
            stage_ref[staged(n, r, c), pl.ds(B, B)] = right[part]
        return carry

    lax.fori_loop(1, GROUPS, prepare, 0)
    my_rows = pl.ds(pl.multiple_of(place(row) * GATHER_ROWS, GATHER_ROWS), GATHER_ROWS)
    my_cols = pl.ds(pl.multiple_of(col * 2 * B, B), 2 * B)
    left, right = pick(row, col)
    for n in range(GATHER_ROUNDS):
        part = slice(n * GATHER_ROWS, (n + 1) * GATHER_ROWS)
        sub_ref[n, my_rows, my_cols] = jnp.concatenate([left[part], right[part]], axis=1)

    pl.semaphore_wait(barrier, GROUPS - 1)

    def send_round(n, carry):
        def send(i, carry):
            r, c = offset_target(i, row, col)
            pltpu.make_async_remote_copy(
                src_ref=stage_ref.at[staged(n, r, c)],
                dst_ref=sub_ref.at[n, my_rows, my_cols],
                send_sem=dsend, recv_sem=drecv.at[n],
                device_id=(r, c), device_id_type=MESH,
            ).start()
            return carry

        return lax.fori_loop(1, GROUPS, send, carry)

    lax.fori_loop(0, GATHER_ROUNDS, send_round, 0)

    my_start = start_of(me)
    my_count = cnt_ref[me]

    for half in range(2):
        pltpu.make_async_copy(phi_ref, phi_ref, phi_sem).wait()

        def turn(at, carry):
            residue = at // 2 + (at % 2) * NCOL
            k = list_place(my_start, residue)
            live = jnp.clip(my_count - k, 0, 1).astype(jnp.float32)
            for t in range(ROWS // 2 // B):
                tile = phi_ref[k, pl.ds(t * B, B), :]
                tile = (tile.astype(jnp.float32) * live).T
                phit_ref[at, :, pl.ds(half * (ROWS // 2) + t * B, B)] = tile.astype(jnp.bfloat16)
            return carry

        lax.fori_loop(0, ENTRIES, turn, 0)
        if half == 0:
            load_phi(1)

    shift = lag(row, col)

    lane = lax.broadcasted_iota(jnp.int32, (GROUPS, GROUPS), 1)
    line = lax.broadcasted_iota(jnp.int32, (GROUPS, GROUPS), 0)
    homes = jnp.broadcast_to(home_row[...], (GROUPS, GROUPS)).T
    starts = jnp.sum(jnp.where(first_row[0:1, :] == line, homes, 0), axis=0, keepdims=True)
    across = jnp.broadcast_to(starts, (GROUPS, GROUPS))
    down = across.T
    ahead = ((across < down) | ((across == down) & (lane < line))).astype(jnp.int32)
    rank = jnp.sum(ahead, axis=1, keepdims=True)
    table_ref[0:1, :] = jnp.sum(jnp.where(rank == lane, line, 0), axis=0, keepdims=True)
    table_ref[1:2, :] = jnp.sum((down < lane).astype(jnp.int32), axis=0, keepdims=True)
    table_ref[2:3, :] = jnp.sum((down < lane + GROUPS).astype(jnp.int32), axis=0, keepdims=True)
    table_ref[3:4, :] = jnp.sum(jnp.where(rank == lane, down, 0), axis=0, keepdims=True)
    tables = pltpu.make_async_copy(table_ref, order_ref, table_sem)
    tables.start()
    tables.wait()

    def below(at):
        return order_ref[1 + at // GROUPS, at % GROUPS]

    def segment(start, apart):
        k = list_place(start, row)
        whole = jnp.clip(ENTRIES - apart - k, 0, 1)
        return ((start + k) >> 4) * 2 + whole

    def keeps(m, carry):
        for at, apart in ((0, shift), (1, NCOL)):
            same = 1 - jnp.clip(segment(order_ref[3, m], apart) - segment(order_ref[3, m - 1], apart), 0, 1)
            keep_ref[at, m] = same.astype(jnp.float32)
        return carry

    keep_ref[0, 0] = 0.0
    keep_ref[1, 0] = 0.0
    lax.fori_loop(1, GROUPS, keeps, 0)
    rho_ref[...] = jnp.zeros_like(rho_ref)

    M, N = ENTRIES * GATHER_ROWS, 256
    one_round = stage_ref.at[pl.ds(0, (GROUPS - 1) * GATHER_ROWS)]

    def density_round(n, carry):
        pltpu.make_async_copy(one_round, one_round, drecv.at[n]).wait()
        rows = pl.ds(pl.multiple_of(n * GATHER_ROWS, GATHER_ROWS), GATHER_ROWS)

        def density(step, carry):
            cols = pl.ds(pl.multiple_of(step * N, N), N)
            g = jnp.dot(
                sub_ref[n], phit_ref[:, :, cols].reshape(WIDTH, N), preferred_element_type=jnp.float32
            )
            g = g * phit_ref[:, rows, cols].reshape(M, N).astype(jnp.float32)
            rho_ref[:, cols] += jnp.sum(g.reshape(M // 8, 8, N), axis=0)
            return carry

        return lax.fori_loop(0, ROWS // N, density, carry)

    lax.fori_loop(0, GATHER_ROUNDS, density_round, 0)

    rho = jnp.sum(rho_ref[...], axis=0, keepdims=True)
    pot_ref[...] = w_ref[...].reshape(1, ROWS) * rho * jnp.exp(jnp.log(1.0 + rho * rho) * (-1.0 / 3.0))

    def weigh(c, carry):
        scaled_ref[c] = (
            phit_ref[pl.ds(c * 2, 2)].reshape(2 * B, ROWS).astype(jnp.float32) * pot_ref[...]
        ).astype(jnp.bfloat16)
        return carry

    lax.fori_loop(0, NCOL, weigh, 0)

    HALF = ENTRIES // 2

    def return_round(n):
        rows = pl.ds(pl.multiple_of(n * RETURN_ROWS, RETURN_ROWS), RETURN_ROWS)

        def potential(step, carry):
            c, half = step // 2, step % 2
            v = lax.dot_general(
                phit_ref[pl.ds(half * HALF, HALF), rows, :].reshape(HALF * RETURN_ROWS, ROWS), scaled_ref[c],
                (((1,), (1,)), ((), ())), preferred_element_type=jnp.float32,
            ).astype(jnp.bfloat16).reshape(HALF, RETURN_ROWS, 2 * B)
            back_ref[n, c * 2, pl.ds(half * HALF, HALF)] = v[:, :, :B]
            back_ref[n, c * 2 + 1, pl.ds(half * HALF, HALF)] = v[:, :, B:]
            return carry

        lax.fori_loop(0, NCOL * 2, potential, 0)

        def main_copy(r, c):
            residue = (r + lag(r, c)) % NROW
            return pltpu.make_async_remote_copy(
                src_ref=back_ref.at[n, place(residue), place(r)],
                dst_ref=main_refs[n].at[me],
                send_sem=msend, recv_sem=mrecv.at[n],
                device_id=(r, c), device_id_type=MESH,
            )

        def far_copy(r, c):
            residue = (r + NCOL) % NROW
            return pltpu.make_async_remote_copy(
                src_ref=back_ref.at[n, place(residue), place(r)],
                dst_ref=far_refs[n].at[me],
                send_sem=fsend, recv_sem=frecv.at[n],
                device_id=(r, c), device_id_type=MESH,
            )

        def give(i, carry):
            r, c = offset_target(i, row, col)
            main_copy(r, c).start()

            @pl.when(keeps_far(r, c))
            def _():
                far_copy(r, c).start()

            return carry

        lax.fori_loop(1, GROUPS, give, 0)
        residue = (row + lag(row, col)) % NROW
        own = pltpu.make_async_copy(back_ref.at[n, place(residue), place(row)], main_refs[n].at[me], self_sem)
        own.start()
        own.wait()

        @pl.when(keeps_far(row, col))
        def _():
            residue = (row + NCOL) % NROW
            own = pltpu.make_async_copy(back_ref.at[n, place(residue), place(row)], far_refs[n].at[me], self_sem)
            own.start()
            own.wait()

    for n in range(RETURN_ROUNDS):
        return_round(n)
    gathered = stage_ref.at[pl.ds(0, (GROUPS - 1) * B)]
    pltpu.make_async_copy(gathered, gathered, dsend).wait()

    def relay_shift(i):
        return (5 * i + 1) % NROW, (3 * i) % NCOL

    def relay(i):
        dr, dc = relay_shift(i)
        return (row + dr) % NROW, (col + dc) % NCOL

    def final(i):
        dr, dc = relay_shift(i)
        return mirror_owner((row - dr + NROW) % NROW, (col - dc + NCOL) % NCOL)

    def first(n, i):
        return pltpu.make_async_remote_copy(
            src_ref=turned_ref.at[n, i], dst_ref=relay_ref.at[n, i], send_sem=send1.at[n, i], recv_sem=recv1.at[n, i],
            device_id=relay(i), device_id_type=MESH,
        )

    def second(n, i):
        return pltpu.make_async_remote_copy(
            src_ref=relay_ref.at[n, i], dst_ref=mirrored_ref.at[n, i], send_sem=send2.at[n, i], recv_sem=recv2.at[n, i],
            device_id=final(i), device_id_type=MESH,
        )

    def stays(i):
        r, c = final(i)
        return r * NCOL + c == me

    def total(parts_ref, n, which, apart, out_ref):
        for u in range(RETURN_ROWS // RUN):
            rows = pl.ds(u * RUN, RUN)

            def add(m, acc):
                acc = acc * keep_ref[which, m] + parts_ref[order_ref[0, m], rows, :].astype(jnp.float32)
                run_ref[m] = acc
                return acc

            lax.fori_loop(0, GROUPS, add, jnp.zeros((RUN, B), jnp.float32))
            out_rows = pl.ds(pl.multiple_of(n * RETURN_ROWS + u * RUN, RUN), RUN)

            def slot(at, carry):
                i, w = at // 2, at % 2

                def ended(i):
                    p = row + i * NROW
                    low = jnp.where(w == 1, p - 15, p - 15 + apart)
                    high = jnp.where(w == 1, p - 15 + apart, p + 1)
                    before = below(jnp.clip(low, 0, GROUPS))
                    until = below(jnp.clip(high, 0, GROUPS))
                    some = jnp.clip(until - before, 0, 1).astype(jnp.float32)
                    return run_ref[jnp.maximum(until - 1, 0)] * some

                out_ref[at, out_rows, :] = ended(i)

                @pl.when(i == 0)
                def _():
                    out_ref[at, out_rows, :] += ended(BLOCK_ROWS)

                return carry

            lax.fori_loop(0, SLOTS, slot, 0)

    one_part = stage_ref.at[pl.ds(0, (GROUPS - 1) * RETURN_ROWS // 2)]

    def finish_round(n):
        pltpu.make_async_copy(one_part, one_part, mrecv.at[n]).wait()
        total(main_refs[n], n, 0, shift, near_ref)

        @pl.when(keeps_far(row, col))
        def _():
            pltpu.make_async_copy(one_part, one_part, frecv.at[n]).wait()
            total(far_refs[n], n, 1, NCOL, wide_ref)

        def start_first(i, carry):
            rows = pl.ds(pl.multiple_of(n * RETURN_ROWS, RETURN_ROWS), RETURN_ROWS)

            @pl.when(keeps_far(row, col))
            def _():
                turned_ref[n, i] = wide_ref[i, rows, :].astype(jnp.bfloat16)

            @pl.when(jnp.logical_not(keeps_far(row, col)))
            def _():
                turned_ref[n, i] = near_ref[i, rows, :].astype(jnp.bfloat16)

            first(n, i).start()
            return carry

        lax.fori_loop(0, SLOTS, start_first, 0)

        def pass_on(i, carry):
            first(n, i).wait_recv()

            @pl.when(jnp.logical_not(stays(i)))
            def _():
                second(n, i).start()

            @pl.when(stays(i))
            def _():
                pltpu.make_async_copy(relay_ref.at[n, i], mirrored_ref.at[n, i], recv2.at[n, i]).start()

            return carry

        lax.fori_loop(0, SLOTS, pass_on, 0)

    @pl.when(jnp.logical_not(keeps_far(row, col)))
    def _():
        wide_ref[...] = jnp.zeros_like(wide_ref)

    for n in range(RETURN_ROUNDS):
        finish_round(n)

    def done(at, carry):
        n, i = at // SLOTS, at % SLOTS
        first(n, i).wait_send()
        second(n, i).wait_recv()

        @pl.when(jnp.logical_not(stays(i)))
        def _():
            second(n, i).wait_send()

        return carry

    lax.fori_loop(0, RETURN_ROUNDS * SLOTS, done, 0)

    sent = stage_ref.at[pl.ds(0, (GROUPS - 1) * B // 2)]
    pltpu.make_async_copy(sent, sent, msend).wait()

    @pl.when(keeps_far(row, col))
    def _():
        others = stage_ref.at[pl.ds(0, (NCOL - 1) * B // 2)]
        pltpu.make_async_copy(others, others, fsend).wait()

    @pl.when(jnp.logical_not(keeps_far(row, col)))
    def _():
        others = stage_ref.at[pl.ds(0, NCOL * B // 2)]
        pltpu.make_async_copy(others, others, fsend).wait()


VMEM = pl.BlockSpec(memory_space=pltpu.VMEM)
SMEM = pl.BlockSpec(memory_space=pltpu.SMEM)
HBM = pl.BlockSpec(memory_space=pl.ANY)


def exchange(lists, home, cnt, w, dens, phi):
    sums = jax.ShapeDtypeStruct((SLOTS, B, B), jnp.float32)
    parts = (GROUPS, RETURN_ROWS, B)
    slots = (RETURN_ROUNDS, SLOTS, RETURN_ROWS, B)
    dma = pltpu.SemaphoreType.DMA
    return pl.pallas_call(
        group_kernel,
        out_shape=[sums, sums, jax.ShapeDtypeStruct(slots, jnp.bfloat16)],
        in_specs=[SMEM, SMEM, VMEM, VMEM, SMEM, VMEM, HBM, HBM],
        out_specs=[VMEM, VMEM, VMEM],
        scratch_shapes=[
            pltpu.VMEM((ENTRIES, BLOCK_ROWS, B, B), jnp.bfloat16),
            pltpu.VMEM((ENTRIES, ROWS // 2, B), jnp.bfloat16),
            pltpu.VMEM((NCOL, 2 * B, ROWS), jnp.bfloat16),
            pltpu.VMEM((ENTRIES, B, ROWS), jnp.bfloat16),
            pltpu.VMEM((GATHER_ROUNDS, ENTRIES * GATHER_ROWS, WIDTH), jnp.bfloat16),
            pltpu.VMEM((GROUPS * B, 2 * B), jnp.bfloat16),
            pltpu.VMEM((RETURN_ROUNDS, ENTRIES, ENTRIES, RETURN_ROWS, B), jnp.bfloat16),
            pltpu.VMEM((8, ROWS), jnp.float32),
            pltpu.VMEM((1, ROWS), jnp.float32),
            [pltpu.VMEM(parts, jnp.bfloat16)] * RETURN_ROUNDS,
            [pltpu.VMEM(parts, jnp.bfloat16)] * RETURN_ROUNDS,
            pltpu.VMEM((GROUPS, RUN, B), jnp.float32),
            pltpu.VMEM(slots, jnp.bfloat16),
            pltpu.VMEM(slots, jnp.bfloat16),
            pltpu.SMEM((2, GROUPS), jnp.float32),
            pltpu.VMEM((8, GROUPS), jnp.int32),
            pltpu.SMEM((8, GROUPS), jnp.int32),
            dma, dma, dma, dma, dma((GATHER_ROUNDS,)), dma, dma((RETURN_ROUNDS,)), dma, dma((RETURN_ROUNDS,)), dma,
        ] + [dma((RETURN_ROUNDS, SLOTS))] * 4,
        compiler_params=pltpu.CompilerParams(
            collective_id=0, has_side_effects=True, vmem_limit_bytes=61 << 20
        ),
        cost_estimate=pl.CostEstimate(flops=4 * ROWS * WIDTH * WIDTH, bytes_accessed=16 << 20, transcendentals=2 * ROWS),
    )(lists, home, lists, home.reshape(1, GROUPS), cnt, w, dens, phi)


def place_kernel(near_ref, wide_ref, mirrored_ref, out_ref):
    row, col = lax.axis_index("row"), lax.axis_index("col")
    i = pl.program_id(0)
    shift = lag(row, col)
    out_ref[...] = jnp.zeros_like(out_ref)
    p = row + NROW * i

    def columns(q):
        return pl.ds(pl.multiple_of(((q & (GROUPS - 1)) >> 3) * B, B), B)

    @pl.when(shift == 0)
    def _():
        out_ref[:, columns(p)] = near_ref[0]

    @pl.when(shift != 0)
    def _():
        for w in range(2):
            out_ref[:, columns(p + shift - NROW * w)] = near_ref[w]

    @pl.when(keeps_far(row, col))
    def _():
        for w in range(2):
            out_ref[:, columns(p + NCOL - NROW * w)] = wide_ref[w]

    @pl.when(jnp.logical_not(keeps_far(row, col)))
    def _():
        for w in range(2):
            there = p - (NCOL - shift) + NROW * w
            at = ((there & (GROUPS - 1)) >> 4) * 2 + w
            block = jnp.concatenate([mirrored_ref[n, at] for n in range(RETURN_ROUNDS)], axis=0)
            out_ref[:, columns(there)] = block.astype(jnp.float32).T


def assemble(near, wide, mirrored):
    def wide_index(i):
        return i * keeps_far(lax.axis_index("row"), lax.axis_index("col")).astype(jnp.int32), 0, 0

    return pl.pallas_call(
        place_kernel,
        grid=(BLOCK_ROWS,),
        out_shape=jax.ShapeDtypeStruct((BLOCK_ROWS * B, WIDTH), jnp.float32),
        in_specs=[
            pl.BlockSpec((2, B, B), lambda i: (i, 0, 0)),
            pl.BlockSpec((2, B, B), wide_index),
            VMEM,
        ],
        out_specs=pl.BlockSpec((B, WIDTH), lambda i: (i, 0)),
    )(near, wide, mirrored)


def body(basis_values, point_weights, density_stored, relevant_blocks, relevant_count, block_home):
    near, wide, mirrored = exchange(
        relevant_blocks.T, block_home, relevant_count, point_weights,
        density_stored.reshape(BLOCK_ROWS, B, WIDTH), basis_values,
    )
    return assemble(near, wide, mirrored)


def solution(mesh):
    in_specs = (P(("row", "col"), None), P(("row", "col")), P("row", "col"), P(), P(), P())
    return jax.shard_map(body, mesh=mesh, in_specs=in_specs, out_specs=P("row", "col"), check_vma=False)
```

```python
import jax
import jax.numpy as jnp
from jax import lax
from jax.experimental import pallas as pl
from jax.experimental.pallas import tpu as pltpu
from jax.sharding import PartitionSpec as P

MESH = pl.DeviceIdType.MESH
NROW, NCOL, GROUPS, B = 16, 8, 128, 128
ENTRIES = 16
ROWS = 1536
WIDTH = ENTRIES * B
BLOCK_ROWS = 8
GATHER_ROUNDS, GATHER_ROWS = 8, 16
RETURN_ROUNDS, RETURN_ROWS = 2, 64
RUN = 32
SLOTS = 2 * BLOCK_ROWS


def place(residue):
    return (residue % NCOL) * 2 + residue // NCOL


def offset_target(step, row, col):
    t = (step * (step + 1) // 2) % GROUPS
    y = (row // 4 + t % 4) % 4
    x = (row % 4 + (t // 4) % 4) % 4
    z = (col // 2 + (t // 16) % 4) % 4
    core = (col + t // 64) % 2
    return y * 4 + x, z * 2 + core


def list_place(start, residue):
    return (residue - start) & (ENTRIES - 1)


def position(start, residue):
    return (start + list_place(start, residue)) & (GROUPS - 1)


def lag(row, col):
    return (col - row + NROW) % NCOL


def keeps_far(row, col):
    return (lag(row, col) == 0) & (row < NCOL)


def mirror_owner(row, col):
    shift = lag(row, col)
    return (row + shift + NCOL * (shift == 0).astype(jnp.int32)) % NROW, row % NCOL


def group_kernel(
    first_ref, home_ref, first_row, home_row, cnt_ref, w_ref, dens_hbm, phi_hbm, near_ref, wide_ref, mirrored_ref,
    dens_ref, phi_ref, scaled_ref, phit_ref, sub_ref, stage_ref, back_ref, rho_ref, pot_ref,
    main_refs, far_refs, run_ref, turned_ref, relay_ref, keep_ref, table_ref, order_ref,
    table_sem, dens_sem, phi_sem, dsend, drecv, msend, mrecv, fsend, frecv, self_sem, send1, recv1, send2, recv2,
):
    row, col = lax.axis_index("row"), lax.axis_index("col")
    me = row * NCOL + col

    def start_of(group):
        return home_ref[first_ref[0, group]]

    def column(k):
        return pl.ds(k * B, B)

    dens_copies = [
        pltpu.make_async_copy(dens_hbm.at[:, :, column(k)], dens_ref.at[k], dens_sem) for k in range(ENTRIES)
    ]
    for copy in dens_copies:
        copy.start()

    def load_phi(half):
        for k in range(ENTRIES):
            pltpu.make_async_copy(
                phi_hbm.at[pl.ds(half * (ROWS // 2), ROWS // 2), column(k)], phi_ref.at[k], phi_sem
            ).start()

    load_phi(0)

    barrier = pltpu.get_barrier_semaphore()

    def greet(i, carry):
        r, c = offset_target(i, row, col)
        pl.semaphore_signal(barrier, inc=1, device_id=(r, c), device_id_type=MESH)
        return carry

    lax.fori_loop(1, GROUPS, greet, 0)

    def pick(r, c):
        start = start_of(r * NCOL + c)
        i = position(start, row) >> 4
        j0 = position(start, col) >> 3
        j1 = position(start, col + NCOL) >> 3
        return dens_ref[j0, i], dens_ref[j1, i]

    pltpu.make_async_copy(dens_ref, dens_ref, dens_sem).wait()

    def staged(n, r, c):
        at = (n * GROUPS + r * NCOL + c) * GATHER_ROWS
        return pl.ds(pl.multiple_of(at, GATHER_ROWS), GATHER_ROWS)

    def prepare(i, carry):
        r, c = offset_target(i, row, col)
        left, right = pick(r, c)
        for n in range(GATHER_ROUNDS):
            part = slice(n * GATHER_ROWS, (n + 1) * GATHER_ROWS)
            stage_ref[staged(n, r, c), pl.ds(0, B)] = left[part]
            stage_ref[staged(n, r, c), pl.ds(B, B)] = right[part]
        return carry

    lax.fori_loop(1, GROUPS, prepare, 0)
    my_rows = pl.ds(pl.multiple_of(place(row) * GATHER_ROWS, GATHER_ROWS), GATHER_ROWS)
    my_cols = pl.ds(pl.multiple_of(col * 2 * B, B), 2 * B)
    left, right = pick(row, col)
    for n in range(GATHER_ROUNDS):
        part = slice(n * GATHER_ROWS, (n + 1) * GATHER_ROWS)
        sub_ref[n, my_rows, my_cols] = jnp.concatenate([left[part], right[part]], axis=1)

    pl.semaphore_wait(barrier, GROUPS - 1)

    def send_round(n, carry):
        def send(i, carry):
            r, c = offset_target(i, row, col)
            pltpu.make_async_remote_copy(
                src_ref=stage_ref.at[staged(n, r, c)],
                dst_ref=sub_ref.at[n, my_rows, my_cols],
                send_sem=dsend, recv_sem=drecv.at[n],
                device_id=(r, c), device_id_type=MESH,
            ).start()
            return carry

        return lax.fori_loop(1, GROUPS, send, carry)

    lax.fori_loop(0, GATHER_ROUNDS, send_round, 0)

    my_start = start_of(me)
    my_count = cnt_ref[me]

    for half in range(2):
        pltpu.make_async_copy(phi_ref, phi_ref, phi_sem).wait()

        def turn(at, carry):
            residue = at // 2 + (at % 2) * NCOL
            k = list_place(my_start, residue)
            live = jnp.clip(my_count - k, 0, 1).astype(jnp.float32)
            for t in range(ROWS // 2 // B):
                tile = phi_ref[k, pl.ds(t * B, B), :]
                tile = (tile.astype(jnp.float32) * live).T
                phit_ref[at, :, pl.ds(half * (ROWS // 2) + t * B, B)] = tile.astype(jnp.bfloat16)
            return carry

        lax.fori_loop(0, ENTRIES, turn, 0)
        if half == 0:
            load_phi(1)

    shift = lag(row, col)

    lane = lax.broadcasted_iota(jnp.int32, (GROUPS, GROUPS), 1)
    line = lax.broadcasted_iota(jnp.int32, (GROUPS, GROUPS), 0)
    homes = jnp.broadcast_to(home_row[...], (GROUPS, GROUPS)).T
    starts = jnp.sum(jnp.where(first_row[0:1, :] == line, homes, 0), axis=0, keepdims=True)
    across = jnp.broadcast_to(starts, (GROUPS, GROUPS))
    down = across.T
    ahead = ((across < down) | ((across == down) & (lane < line))).astype(jnp.int32)
    rank = jnp.sum(ahead, axis=1, keepdims=True)
    table_ref[0:1, :] = jnp.sum(jnp.where(rank == lane, line, 0), axis=0, keepdims=True)
    table_ref[1:2, :] = jnp.sum((down < lane).astype(jnp.int32), axis=0, keepdims=True)
    table_ref[2:3, :] = jnp.sum((down < lane + GROUPS).astype(jnp.int32), axis=0, keepdims=True)
    table_ref[3:4, :] = jnp.sum(jnp.where(rank == lane, down, 0), axis=0, keepdims=True)
    tables = pltpu.make_async_copy(table_ref, order_ref, table_sem)
    tables.start()
    tables.wait()

    def below(at):
        return order_ref[1 + at // GROUPS, at % GROUPS]

    def segment(start, apart):
        k = list_place(start, row)
        whole = jnp.clip(ENTRIES - apart - k, 0, 1)
        return ((start + k) >> 4) * 2 + whole

    def keeps(m, carry):
        for at, apart in ((0, shift), (1, NCOL)):
            same = 1 - jnp.clip(segment(order_ref[3, m], apart) - segment(order_ref[3, m - 1], apart), 0, 1)
            keep_ref[at, m] = same.astype(jnp.float32)
        return carry

    keep_ref[0, 0] = 0.0
    keep_ref[1, 0] = 0.0
    lax.fori_loop(1, GROUPS, keeps, 0)
    rho_ref[...] = jnp.zeros_like(rho_ref)

    M, N = ENTRIES * GATHER_ROWS, 256
    one_round = stage_ref.at[pl.ds(0, (GROUPS - 1) * GATHER_ROWS)]

    def density_round(n, carry):
        pltpu.make_async_copy(one_round, one_round, drecv.at[n]).wait()
        rows = pl.ds(pl.multiple_of(n * GATHER_ROWS, GATHER_ROWS), GATHER_ROWS)

        def density(step, carry):
            cols = pl.ds(pl.multiple_of(step * N, N), N)
            g = jnp.dot(
                sub_ref[n], phit_ref[:, :, cols].reshape(WIDTH, N), preferred_element_type=jnp.float32
            )
            g = g * phit_ref[:, rows, cols].reshape(M, N).astype(jnp.float32)
            rho_ref[:, cols] += jnp.sum(g.reshape(M // 8, 8, N), axis=0)
            return carry

        return lax.fori_loop(0, ROWS // N, density, carry)

    lax.fori_loop(0, GATHER_ROUNDS, density_round, 0)

    rho = jnp.sum(rho_ref[...], axis=0, keepdims=True)
    pot_ref[...] = w_ref[...].reshape(1, ROWS) * rho * jnp.exp(jnp.log(1.0 + rho * rho) * (-1.0 / 3.0))

    def weigh(c, carry):
        scaled_ref[c] = (
            phit_ref[pl.ds(c * 2, 2)].reshape(2 * B, ROWS).astype(jnp.float32) * pot_ref[...]
        ).astype(jnp.bfloat16)
        return carry

    lax.fori_loop(0, NCOL, weigh, 0)

    HALF = ENTRIES // 2

    def return_round(n):
        rows = pl.ds(pl.multiple_of(n * RETURN_ROWS, RETURN_ROWS), RETURN_ROWS)

        def potential(step, carry):
            c, half = step // 2, step % 2
            v = lax.dot_general(
                phit_ref[pl.ds(half * HALF, HALF), rows, :].reshape(HALF * RETURN_ROWS, ROWS), scaled_ref[c],
                (((1,), (1,)), ((), ())), preferred_element_type=jnp.float32,
            ).astype(jnp.bfloat16).reshape(HALF, RETURN_ROWS, 2 * B)
            back_ref[n, c * 2, pl.ds(half * HALF, HALF)] = v[:, :, :B]
            back_ref[n, c * 2 + 1, pl.ds(half * HALF, HALF)] = v[:, :, B:]
            return carry

        lax.fori_loop(0, NCOL * 2, potential, 0)

        def main_copy(r, c):
            residue = (r + lag(r, c)) % NROW
            return pltpu.make_async_remote_copy(
                src_ref=back_ref.at[n, place(residue), place(r)],
                dst_ref=main_refs[n].at[me],
                send_sem=msend, recv_sem=mrecv.at[n],
                device_id=(r, c), device_id_type=MESH,
            )

        def far_copy(r, c):
            residue = (r + NCOL) % NROW
            return pltpu.make_async_remote_copy(
                src_ref=back_ref.at[n, place(residue), place(r)],
                dst_ref=far_refs[n].at[me],
                send_sem=fsend, recv_sem=frecv.at[n],
                device_id=(r, c), device_id_type=MESH,
            )

        def give(i, carry):
            r, c = offset_target(i, row, col)
            main_copy(r, c).start()

            @pl.when(keeps_far(r, c))
            def _():
                far_copy(r, c).start()

            return carry

        lax.fori_loop(1, GROUPS, give, 0)
        residue = (row + lag(row, col)) % NROW
        own = pltpu.make_async_copy(back_ref.at[n, place(residue), place(row)], main_refs[n].at[me], self_sem)
        own.start()
        own.wait()

        @pl.when(keeps_far(row, col))
        def _():
            residue = (row + NCOL) % NROW
            own = pltpu.make_async_copy(back_ref.at[n, place(residue), place(row)], far_refs[n].at[me], self_sem)
            own.start()
            own.wait()

    for n in range(RETURN_ROUNDS):
        return_round(n)
    gathered = stage_ref.at[pl.ds(0, (GROUPS - 1) * B)]
    pltpu.make_async_copy(gathered, gathered, dsend).wait()

    def relay_shift(i):
        return (5 * i + 1) % NROW, (3 * i) % NCOL

    def relay(i):
        dr, dc = relay_shift(i)
        return (row + dr) % NROW, (col + dc) % NCOL

    def final(i):
        dr, dc = relay_shift(i)
        return mirror_owner((row - dr + NROW) % NROW, (col - dc + NCOL) % NCOL)

    def first(n, i):
        return pltpu.make_async_remote_copy(
            src_ref=turned_ref.at[n, i], dst_ref=relay_ref.at[n, i], send_sem=send1.at[n, i], recv_sem=recv1.at[n, i],
            device_id=relay(i), device_id_type=MESH,
        )

    def second(n, i):
        return pltpu.make_async_remote_copy(
            src_ref=relay_ref.at[n, i], dst_ref=mirrored_ref.at[n, i], send_sem=send2.at[n, i], recv_sem=recv2.at[n, i],
            device_id=final(i), device_id_type=MESH,
        )

    def stays(i):
        r, c = final(i)
        return r * NCOL + c == me

    def total(parts_ref, n, which, apart, out_ref):
        for u in range(RETURN_ROWS // RUN):
            rows = pl.ds(u * RUN, RUN)

            def add(m, acc):
                acc = acc * keep_ref[which, m] + parts_ref[order_ref[0, m], rows, :].astype(jnp.float32)
                run_ref[m] = acc
                return acc

            lax.fori_loop(0, GROUPS, add, jnp.zeros((RUN, B), jnp.float32), unroll=8)
            out_rows = pl.ds(pl.multiple_of(n * RETURN_ROWS + u * RUN, RUN), RUN)

            def slot(at, carry):
                i, w = at // 2, at % 2

                def ended(i):
                    p = row + i * NROW
                    low = jnp.where(w == 1, p - 15, p - 15 + apart)
                    high = jnp.where(w == 1, p - 15 + apart, p + 1)
                    before = below(jnp.clip(low, 0, GROUPS))
                    until = below(jnp.clip(high, 0, GROUPS))
                    some = jnp.clip(until - before, 0, 1).astype(jnp.float32)
                    return run_ref[jnp.maximum(until - 1, 0)] * some

                out_ref[at, out_rows, :] = ended(i)

                @pl.when(i == 0)
                def _():
                    out_ref[at, out_rows, :] += ended(BLOCK_ROWS)

                return carry

            lax.fori_loop(0, SLOTS, slot, 0)

    one_part = stage_ref.at[pl.ds(0, (GROUPS - 1) * RETURN_ROWS // 2)]

    def finish_round(n):
        def total_near():
            pltpu.make_async_copy(one_part, one_part, mrecv.at[n]).wait()
            total(main_refs[n], n, 0, shift, near_ref)

        pl.when(jnp.logical_not(keeps_far(row, col)))(total_near)

        @pl.when(keeps_far(row, col))
        def _():
            pltpu.make_async_copy(one_part, one_part, frecv.at[n]).wait()
            total(far_refs[n], n, 1, NCOL, wide_ref)

        def start_first(i, carry):
            rows = pl.ds(pl.multiple_of(n * RETURN_ROWS, RETURN_ROWS), RETURN_ROWS)

            @pl.when(keeps_far(row, col))
            def _():
                turned_ref[n, i] = wide_ref[i, rows, :].astype(jnp.bfloat16)

            @pl.when(jnp.logical_not(keeps_far(row, col)))
            def _():
                turned_ref[n, i] = near_ref[i, rows, :].astype(jnp.bfloat16)

            first(n, i).start()
            return carry

        lax.fori_loop(0, SLOTS, start_first, 0)

        def pass_on(i, carry):
            first(n, i).wait_recv()

            @pl.when(jnp.logical_not(stays(i)))
            def _():
                second(n, i).start()

            @pl.when(stays(i))
            def _():
                pltpu.make_async_copy(relay_ref.at[n, i], mirrored_ref.at[n, i], recv2.at[n, i]).start()

            return carry

        lax.fori_loop(0, SLOTS, pass_on, 0)
        pl.when(keeps_far(row, col))(total_near)

    @pl.when(jnp.logical_not(keeps_far(row, col)))
    def _():
        wide_ref[...] = jnp.zeros_like(wide_ref)

    for n in range(RETURN_ROUNDS):
        finish_round(n)

    def done(at, carry):
        n, i = at // SLOTS, at % SLOTS
        first(n, i).wait_send()
        second(n, i).wait_recv()

        @pl.when(jnp.logical_not(stays(i)))
        def _():
            second(n, i).wait_send()

        return carry

    lax.fori_loop(0, RETURN_ROUNDS * SLOTS, done, 0)

    sent = stage_ref.at[pl.ds(0, (GROUPS - 1) * B // 2)]
    pltpu.make_async_copy(sent, sent, msend).wait()

    @pl.when(keeps_far(row, col))
    def _():
        others = stage_ref.at[pl.ds(0, (NCOL - 1) * B // 2)]
        pltpu.make_async_copy(others, others, fsend).wait()

    @pl.when(jnp.logical_not(keeps_far(row, col)))
    def _():
        others = stage_ref.at[pl.ds(0, NCOL * B // 2)]
        pltpu.make_async_copy(others, others, fsend).wait()


VMEM = pl.BlockSpec(memory_space=pltpu.VMEM)
SMEM = pl.BlockSpec(memory_space=pltpu.SMEM)
HBM = pl.BlockSpec(memory_space=pl.ANY)


def exchange(lists, home, cnt, w, dens, phi):
    sums = jax.ShapeDtypeStruct((SLOTS, B, B), jnp.float32)
    parts = (GROUPS, RETURN_ROWS, B)
    slots = (RETURN_ROUNDS, SLOTS, RETURN_ROWS, B)
    dma = pltpu.SemaphoreType.DMA
    return pl.pallas_call(
        group_kernel,
        out_shape=[sums, sums, jax.ShapeDtypeStruct(slots, jnp.bfloat16)],
        in_specs=[SMEM, SMEM, VMEM, VMEM, SMEM, VMEM, HBM, HBM],
        out_specs=[VMEM, VMEM, VMEM],
        scratch_shapes=[
            pltpu.VMEM((ENTRIES, BLOCK_ROWS, B, B), jnp.bfloat16),
            pltpu.VMEM((ENTRIES, ROWS // 2, B), jnp.bfloat16),
            pltpu.VMEM((NCOL, 2 * B, ROWS), jnp.bfloat16),
            pltpu.VMEM((ENTRIES, B, ROWS), jnp.bfloat16),
            pltpu.VMEM((GATHER_ROUNDS, ENTRIES * GATHER_ROWS, WIDTH), jnp.bfloat16),
            pltpu.VMEM((GROUPS * B, 2 * B), jnp.bfloat16),
            pltpu.VMEM((RETURN_ROUNDS, ENTRIES, ENTRIES, RETURN_ROWS, B), jnp.bfloat16),
            pltpu.VMEM((8, ROWS), jnp.float32),
            pltpu.VMEM((1, ROWS), jnp.float32),
            [pltpu.VMEM(parts, jnp.bfloat16)] * RETURN_ROUNDS,
            [pltpu.VMEM(parts, jnp.bfloat16)] * RETURN_ROUNDS,
            pltpu.VMEM((GROUPS, RUN, B), jnp.float32),
            pltpu.VMEM(slots, jnp.bfloat16),
            pltpu.VMEM(slots, jnp.bfloat16),
            pltpu.SMEM((2, GROUPS), jnp.float32),
            pltpu.VMEM((8, GROUPS), jnp.int32),
            pltpu.SMEM((8, GROUPS), jnp.int32),
            dma, dma, dma, dma, dma((GATHER_ROUNDS,)), dma, dma((RETURN_ROUNDS,)), dma, dma((RETURN_ROUNDS,)), dma,
        ] + [dma((RETURN_ROUNDS, SLOTS))] * 4,
        compiler_params=pltpu.CompilerParams(
            collective_id=0, has_side_effects=True, vmem_limit_bytes=61 << 20
        ),
        cost_estimate=pl.CostEstimate(flops=4 * ROWS * WIDTH * WIDTH, bytes_accessed=16 << 20, transcendentals=2 * ROWS),
    )(lists, home, lists, home.reshape(1, GROUPS), cnt, w, dens, phi)


def place_kernel(near_hbm, wide_hbm, mirrored_hbm, out_hbm, near_ref, wide_ref, mirrored_ref, rows_ref, in_sem, out_sem):
    row, col = lax.axis_index("row"), lax.axis_index("col")
    shift = lag(row, col)
    near_copy = pltpu.make_async_copy(near_hbm, near_ref, in_sem.at[0])
    wide_copy = pltpu.make_async_copy(wide_hbm, wide_ref, in_sem.at[1])
    mirrored_copy = pltpu.make_async_copy(mirrored_hbm, mirrored_ref, in_sem.at[2])
    for copy in (near_copy, wide_copy, mirrored_copy):
        copy.start()

    def clear(i, carry):
        rows_ref[i] = jnp.zeros((B, WIDTH), jnp.float32)
        return carry

    lax.fori_loop(0, BLOCK_ROWS, clear, 0)
    for copy in (near_copy, wide_copy, mirrored_copy):
        copy.wait()

    def columns(q):
        return pl.ds(pl.multiple_of(((q & (GROUPS - 1)) >> 3) * B, B), B)

    def out_copy(i):
        return pltpu.make_async_copy(rows_ref.at[i], out_hbm.at[i], out_sem.at[i])

    def fill(i, carry):
        p = row + NROW * i

        @pl.when(shift == 0)
        def _():
            rows_ref[i, :, columns(p)] = near_ref[i * 2]

        @pl.when(shift != 0)
        def _():
            for w in range(2):
                rows_ref[i, :, columns(p + shift - NROW * w)] = near_ref[i * 2 + w]

        @pl.when(keeps_far(row, col))
        def _():
            for w in range(2):
                rows_ref[i, :, columns(p + NCOL - NROW * w)] = wide_ref[i * 2 + w]

        @pl.when(jnp.logical_not(keeps_far(row, col)))
        def _():
            for w in range(2):
                there = p - (NCOL - shift) + NROW * w
                at = ((there & (GROUPS - 1)) >> 4) * 2 + w
                block = jnp.concatenate([mirrored_ref[n, at] for n in range(RETURN_ROUNDS)], axis=0)
                rows_ref[i, :, columns(there)] = block.astype(jnp.float32).T

        out_copy(i).start()
        return carry

    lax.fori_loop(0, BLOCK_ROWS, fill, 0)

    def drain(i, carry):
        out_copy(i).wait()
        return carry

    lax.fori_loop(0, BLOCK_ROWS, drain, 0)


def assemble(near, wide, mirrored):
    return pl.pallas_call(
        place_kernel,
        out_shape=jax.ShapeDtypeStruct((BLOCK_ROWS, B, WIDTH), jnp.float32),
        in_specs=[HBM] * 3,
        out_specs=HBM,
        scratch_shapes=[
            pltpu.VMEM((SLOTS, B, B), jnp.float32),
            pltpu.VMEM((SLOTS, B, B), jnp.float32),
            pltpu.VMEM((RETURN_ROUNDS, SLOTS, RETURN_ROWS, B), jnp.bfloat16),
            pltpu.VMEM((BLOCK_ROWS, B, WIDTH), jnp.float32),
            pltpu.SemaphoreType.DMA((3,)),
            pltpu.SemaphoreType.DMA((BLOCK_ROWS,)),
        ],
        compiler_params=pltpu.CompilerParams(vmem_limit_bytes=32 << 20),
    )(near, wide, mirrored).reshape(BLOCK_ROWS * B, WIDTH)


def body(basis_values, point_weights, density_stored, relevant_blocks, relevant_count, block_home):
    near, wide, mirrored = exchange(
        relevant_blocks.T, block_home, relevant_count, point_weights,
        density_stored.reshape(BLOCK_ROWS, B, WIDTH), basis_values,
    )
    return assemble(near, wide, mirrored)


def solution(mesh):
    in_specs = (P(("row", "col"), None), P(("row", "col")), P("row", "col"), P(), P(), P())
    return jax.shard_map(body, mesh=mesh, in_specs=in_specs, out_specs=P("row", "col"), check_vma=False)
```

```python
import jax
import jax.numpy as jnp
from jax import lax
from jax.experimental import pallas as pl
from jax.experimental.pallas import tpu as pltpu
from jax.sharding import PartitionSpec as P

MESH = pl.DeviceIdType.MESH
NROW, NCOL, GROUPS, B = 16, 8, 128, 128
ENTRIES = 16
ROWS = 1536
WIDTH = ENTRIES * B
BLOCK_ROWS = 8
GATHER_ROUNDS, GATHER_ROWS = 8, 16
RETURN_ROUNDS, RETURN_ROWS = 2, 64
RUN = 32
SLOTS = 2 * BLOCK_ROWS


def place(residue):
    return (residue % NCOL) * 2 + residue // NCOL


def offset_target(step, row, col):
    t = (step * (step + 1) // 2) % GROUPS
    y = (row // 4 + t % 4) % 4
    x = (row % 4 + (t // 4) % 4) % 4
    z = (col // 2 + (t // 16) % 4) % 4
    core = (col + t // 64) % 2
    return y * 4 + x, z * 2 + core


def list_place(start, residue):
    return (residue - start) & (ENTRIES - 1)


def position(start, residue):
    return (start + list_place(start, residue)) & (GROUPS - 1)


def lag(row, col):
    return (col - row + NROW) % NCOL


def keeps_far(row, col):
    return (lag(row, col) == 0) & (row < NCOL)


def mirror_owner(row, col):
    shift = lag(row, col)
    return (row + shift + NCOL * (shift == 0).astype(jnp.int32)) % NROW, row % NCOL


def group_kernel(
    first_ref, home_ref, first_row, home_row, cnt_ref, w_ref, dens_hbm, phi_hbm, near_ref, wide_ref, mirrored_ref,
    dens_ref, phi_ref, scaled_ref, phit_ref, sub_ref, stage_ref, back_ref, rho_ref, pot_ref,
    main_refs, far_refs, run_ref, turned_ref, relay_ref, keep_ref, table_ref, order_ref,
    table_sem, dens_sem, phi_sem, dsend, drecv, msend, mrecv, fsend, frecv, self_sem, send1, recv1, send2, recv2,
):
    row, col = lax.axis_index("row"), lax.axis_index("col")
    me = row * NCOL + col

    def start_of(group):
        return home_ref[first_ref[0, group]]

    def column(k):
        return pl.ds(k * B, B)

    dens_copies = [
        pltpu.make_async_copy(dens_hbm.at[:, :, column(k)], dens_ref.at[k], dens_sem) for k in range(ENTRIES)
    ]
    for copy in dens_copies:
        copy.start()

    def load_phi(half):
        for k in range(ENTRIES):
            pltpu.make_async_copy(
                phi_hbm.at[pl.ds(half * (ROWS // 2), ROWS // 2), column(k)], phi_ref.at[k], phi_sem
            ).start()

    load_phi(0)

    barrier = pltpu.get_barrier_semaphore()

    def greet(i, carry):
        r, c = offset_target(i, row, col)
        pl.semaphore_signal(barrier, inc=1, device_id=(r, c), device_id_type=MESH)
        return carry

    lax.fori_loop(1, GROUPS, greet, 0)

    def pick(r, c):
        start = start_of(r * NCOL + c)
        i = position(start, row) >> 4
        j0 = position(start, col) >> 3
        j1 = position(start, col + NCOL) >> 3
        return dens_ref[j0, i], dens_ref[j1, i]

    pltpu.make_async_copy(dens_ref, dens_ref, dens_sem).wait()

    def staged(n, r, c):
        at = (n * GROUPS + r * NCOL + c) * GATHER_ROWS
        return pl.ds(pl.multiple_of(at, GATHER_ROWS), GATHER_ROWS)

    def prepare(i, carry):
        r, c = offset_target(i, row, col)
        left, right = pick(r, c)
        for n in range(GATHER_ROUNDS):
            part = slice(n * GATHER_ROWS, (n + 1) * GATHER_ROWS)
            stage_ref[staged(n, r, c), pl.ds(0, B)] = left[part]
            stage_ref[staged(n, r, c), pl.ds(B, B)] = right[part]
        return carry

    lax.fori_loop(1, GROUPS, prepare, 0)
    my_rows = pl.ds(pl.multiple_of(place(row) * GATHER_ROWS, GATHER_ROWS), GATHER_ROWS)
    my_cols = pl.ds(pl.multiple_of(col * 2 * B, B), 2 * B)
    left, right = pick(row, col)
    for n in range(GATHER_ROUNDS):
        part = slice(n * GATHER_ROWS, (n + 1) * GATHER_ROWS)
        sub_ref[n, my_rows, my_cols] = jnp.concatenate([left[part], right[part]], axis=1)

    pl.semaphore_wait(barrier, GROUPS - 1)

    def send_round(n, carry):
        def send(i, carry):
            r, c = offset_target(i, row, col)
            pltpu.make_async_remote_copy(
                src_ref=stage_ref.at[staged(n, r, c)],
                dst_ref=sub_ref.at[n, my_rows, my_cols],
                send_sem=dsend, recv_sem=drecv.at[n],
                device_id=(r, c), device_id_type=MESH,
            ).start()
            return carry

        return lax.fori_loop(1, GROUPS, send, carry)

    lax.fori_loop(0, GATHER_ROUNDS, send_round, 0)

    my_start = start_of(me)
    my_count = cnt_ref[me]

    for half in range(2):
        pltpu.make_async_copy(phi_ref, phi_ref, phi_sem).wait()

        def turn(at, carry):
            residue = at // 2 + (at % 2) * NCOL
            k = list_place(my_start, residue)
            live = jnp.clip(my_count - k, 0, 1).astype(jnp.float32)
            for t in range(ROWS // 2 // B):
                tile = phi_ref[k, pl.ds(t * B, B), :]
                tile = (tile.astype(jnp.float32) * live).T
                phit_ref[at, :, pl.ds(half * (ROWS // 2) + t * B, B)] = tile.astype(jnp.bfloat16)
            return carry

        lax.fori_loop(0, ENTRIES, turn, 0)
        if half == 0:
            load_phi(1)

    shift = lag(row, col)

    lane = lax.broadcasted_iota(jnp.int32, (GROUPS, GROUPS), 1)
    line = lax.broadcasted_iota(jnp.int32, (GROUPS, GROUPS), 0)
    homes = jnp.broadcast_to(home_row[...], (GROUPS, GROUPS)).T
    starts = jnp.sum(jnp.where(first_row[0:1, :] == line, homes, 0), axis=0, keepdims=True)
    across = jnp.broadcast_to(starts, (GROUPS, GROUPS))
    down = across.T
    ahead = ((across < down) | ((across == down) & (lane < line))).astype(jnp.int32)
    rank = jnp.sum(ahead, axis=1, keepdims=True)
    table_ref[0:1, :] = jnp.sum(jnp.where(rank == lane, line, 0), axis=0, keepdims=True)
    table_ref[1:2, :] = jnp.sum((down < lane).astype(jnp.int32), axis=0, keepdims=True)
    table_ref[2:3, :] = jnp.sum((down < lane + GROUPS).astype(jnp.int32), axis=0, keepdims=True)
    table_ref[3:4, :] = jnp.sum(jnp.where(rank == lane, down, 0), axis=0, keepdims=True)
    tables = pltpu.make_async_copy(table_ref, order_ref, table_sem)
    tables.start()
    tables.wait()

    def below(at):
        return order_ref[1 + at // GROUPS, at % GROUPS]

    def segment(start, apart):
        k = list_place(start, row)
        whole = jnp.clip(ENTRIES - apart - k, 0, 1)
        return ((start + k) >> 4) * 2 + whole

    def keeps(m, carry):
        for at, apart in ((0, shift), (1, NCOL)):
            same = 1 - jnp.clip(segment(order_ref[3, m], apart) - segment(order_ref[3, m - 1], apart), 0, 1)
            keep_ref[at, m] = same.astype(jnp.float32)
        return carry

    keep_ref[0, 0] = 0.0
    keep_ref[1, 0] = 0.0
    lax.fori_loop(1, GROUPS, keeps, 0)
    rho_ref[...] = jnp.zeros_like(rho_ref)

    M, N = ENTRIES * GATHER_ROWS, 256
    one_round = stage_ref.at[pl.ds(0, (GROUPS - 1) * GATHER_ROWS)]

    def density_round(n, carry):
        pltpu.make_async_copy(one_round, one_round, drecv.at[n]).wait()
        rows = pl.ds(pl.multiple_of(n * GATHER_ROWS, GATHER_ROWS), GATHER_ROWS)

        def density(step, carry):
            cols = pl.ds(pl.multiple_of(step * N, N), N)
            g = jnp.dot(
                sub_ref[n], phit_ref[:, :, cols].reshape(WIDTH, N), preferred_element_type=jnp.float32
            )
            g = g * phit_ref[:, rows, cols].reshape(M, N).astype(jnp.float32)
            rho_ref[:, cols] += jnp.sum(g.reshape(M // 8, 8, N), axis=0)
            return carry

        return lax.fori_loop(0, ROWS // N, density, carry)

    lax.fori_loop(0, GATHER_ROUNDS, density_round, 0)

    rho = jnp.sum(rho_ref[...], axis=0, keepdims=True)
    pot_ref[...] = w_ref[...].reshape(1, ROWS) * rho * jnp.exp(jnp.log(1.0 + rho * rho) * (-1.0 / 3.0))

    def weigh(c, carry):
        scaled_ref[c] = (
            phit_ref[pl.ds(c * 2, 2)].reshape(2 * B, ROWS).astype(jnp.float32) * pot_ref[...]
        ).astype(jnp.bfloat16)
        return carry

    lax.fori_loop(0, NCOL, weigh, 0)

    HALF = ENTRIES // 2

    def return_round(n):
        rows = pl.ds(pl.multiple_of(n * RETURN_ROWS, RETURN_ROWS), RETURN_ROWS)

        def potential(step, carry):
            c, half = step // 2, step % 2
            v = lax.dot_general(
                phit_ref[pl.ds(half * HALF, HALF), rows, :].reshape(HALF * RETURN_ROWS, ROWS), scaled_ref[c],
                (((1,), (1,)), ((), ())), preferred_element_type=jnp.float32,
            ).astype(jnp.bfloat16).reshape(HALF, RETURN_ROWS, 2 * B)
            back_ref[n, c * 2, pl.ds(half * HALF, HALF)] = v[:, :, :B]
            back_ref[n, c * 2 + 1, pl.ds(half * HALF, HALF)] = v[:, :, B:]
            return carry

        lax.fori_loop(0, NCOL * 2, potential, 0)

        def main_copy(r, c):
            residue = (r + lag(r, c)) % NROW
            return pltpu.make_async_remote_copy(
                src_ref=back_ref.at[n, place(residue), place(r)],
                dst_ref=main_refs[n].at[me],
                send_sem=msend, recv_sem=mrecv.at[n],
                device_id=(r, c), device_id_type=MESH,
            )

        def far_copy(r, c):
            residue = (r + NCOL) % NROW
            return pltpu.make_async_remote_copy(
                src_ref=back_ref.at[n, place(residue), place(r)],
                dst_ref=far_refs[n].at[me],
                send_sem=fsend, recv_sem=frecv.at[n],
                device_id=(r, c), device_id_type=MESH,
            )

        def give(i, carry):
            r, c = offset_target(i, row, col)
            main_copy(r, c).start()

            @pl.when(keeps_far(r, c))
            def _():
                far_copy(r, c).start()

            return carry

        lax.fori_loop(1, GROUPS, give, 0)
        residue = (row + lag(row, col)) % NROW
        own = pltpu.make_async_copy(back_ref.at[n, place(residue), place(row)], main_refs[n].at[me], self_sem)
        own.start()
        own.wait()

        @pl.when(keeps_far(row, col))
        def _():
            residue = (row + NCOL) % NROW
            own = pltpu.make_async_copy(back_ref.at[n, place(residue), place(row)], far_refs[n].at[me], self_sem)
            own.start()
            own.wait()

    for n in range(RETURN_ROUNDS):
        return_round(n)
    gathered = stage_ref.at[pl.ds(0, (GROUPS - 1) * B)]
    pltpu.make_async_copy(gathered, gathered, dsend).wait()

    def relay_shift(i):
        return (5 * i + 1) % NROW, (3 * i) % NCOL

    def relay(i):
        dr, dc = relay_shift(i)
        return (row + dr) % NROW, (col + dc) % NCOL

    def final(i):
        dr, dc = relay_shift(i)
        return mirror_owner((row - dr + NROW) % NROW, (col - dc + NCOL) % NCOL)

    def first(n, i):
        return pltpu.make_async_remote_copy(
            src_ref=turned_ref.at[n, i], dst_ref=relay_ref.at[n, i], send_sem=send1.at[n, i], recv_sem=recv1.at[n, i],
            device_id=relay(i), device_id_type=MESH,
        )

    def second(n, i):
        return pltpu.make_async_remote_copy(
            src_ref=relay_ref.at[n, i], dst_ref=mirrored_ref.at[n, i], send_sem=send2.at[n, i], recv_sem=recv2.at[n, i],
            device_id=final(i), device_id_type=MESH,
        )

    def stays(i):
        r, c = final(i)
        return r * NCOL + c == me

    def total(parts_ref, n, which, apart, out_ref):
        for u in range(RETURN_ROWS // RUN):
            rows = pl.ds(u * RUN, RUN)

            def add(m, acc):
                acc = acc * keep_ref[which, m] + parts_ref[order_ref[0, m], rows, :].astype(jnp.float32)
                run_ref[m] = acc
                return acc

            lax.fori_loop(0, GROUPS, add, jnp.zeros((RUN, B), jnp.float32), unroll=8)
            out_rows = pl.ds(pl.multiple_of(n * RETURN_ROWS + u * RUN, RUN), RUN)

            def slot(at, carry):
                i, w = at // 2, at % 2

                def ended(i):
                    p = row + i * NROW
                    low = jnp.where(w == 1, p - 15, p - 15 + apart)
                    high = jnp.where(w == 1, p - 15 + apart, p + 1)
                    before = below(jnp.clip(low, 0, GROUPS))
                    until = below(jnp.clip(high, 0, GROUPS))
                    some = jnp.clip(until - before, 0, 1).astype(jnp.float32)
                    return run_ref[jnp.maximum(until - 1, 0)] * some

                out_ref[at, out_rows, :] = ended(i)

                @pl.when(i == 0)
                def _():
                    out_ref[at, out_rows, :] += ended(BLOCK_ROWS)

                return carry

            lax.fori_loop(0, SLOTS, slot, 0)

    one_part = stage_ref.at[pl.ds(0, (GROUPS - 1) * RETURN_ROWS // 2)]

    def finish_round(n):
        def total_near():
            pltpu.make_async_copy(one_part, one_part, mrecv.at[n]).wait()
            total(main_refs[n], n, 0, shift, near_ref)

        pl.when(jnp.logical_not(keeps_far(row, col)))(total_near)

        @pl.when(keeps_far(row, col))
        def _():
            pltpu.make_async_copy(one_part, one_part, frecv.at[n]).wait()
            total(far_refs[n], n, 1, NCOL, wide_ref)

        def start_first(i, carry):
            rows = pl.ds(pl.multiple_of(n * RETURN_ROWS, RETURN_ROWS), RETURN_ROWS)

            @pl.when(keeps_far(row, col))
            def _():
                turned_ref[n, i] = wide_ref[i, rows, :].astype(jnp.bfloat16)

            @pl.when(jnp.logical_not(keeps_far(row, col)))
            def _():
                turned_ref[n, i] = near_ref[i, rows, :].astype(jnp.bfloat16)

            first(n, i).start()
            return carry

        lax.fori_loop(0, SLOTS, start_first, 0)

        def pass_on(i, carry):
            first(n, i).wait_recv()

            @pl.when(jnp.logical_not(stays(i)))
            def _():
                second(n, i).start()

            @pl.when(stays(i))
            def _():
                pltpu.make_async_copy(relay_ref.at[n, i], mirrored_ref.at[n, i], recv2.at[n, i]).start()

            return carry

        lax.fori_loop(0, SLOTS, pass_on, 0)
        pl.when(keeps_far(row, col))(total_near)

    @pl.when(jnp.logical_not(keeps_far(row, col)))
    def _():
        wide_ref[...] = jnp.zeros_like(wide_ref)

    for n in range(RETURN_ROUNDS):
        finish_round(n)

    def done(at, carry):
        n, i = at // SLOTS, at % SLOTS
        first(n, i).wait_send()
        second(n, i).wait_recv()

        @pl.when(jnp.logical_not(stays(i)))
        def _():
            second(n, i).wait_send()

        return carry

    lax.fori_loop(0, RETURN_ROUNDS * SLOTS, done, 0)

    sent = stage_ref.at[pl.ds(0, (GROUPS - 1) * B // 2)]
    pltpu.make_async_copy(sent, sent, msend).wait()

    @pl.when(keeps_far(row, col))
    def _():
        others = stage_ref.at[pl.ds(0, (NCOL - 1) * B // 2)]
        pltpu.make_async_copy(others, others, fsend).wait()

    @pl.when(jnp.logical_not(keeps_far(row, col)))
    def _():
        others = stage_ref.at[pl.ds(0, NCOL * B // 2)]
        pltpu.make_async_copy(others, others, fsend).wait()


VMEM = pl.BlockSpec(memory_space=pltpu.VMEM)
SMEM = pl.BlockSpec(memory_space=pltpu.SMEM)
HBM = pl.BlockSpec(memory_space=pl.ANY)


def exchange(lists, home, cnt, w, dens, phi):
    sums = jax.ShapeDtypeStruct((SLOTS, B, B), jnp.float32)
    parts = (GROUPS, RETURN_ROWS, B)
    slots = (RETURN_ROUNDS, SLOTS, RETURN_ROWS, B)
    dma = pltpu.SemaphoreType.DMA
    return pl.pallas_call(
        group_kernel,
        out_shape=[sums, sums, jax.ShapeDtypeStruct(slots, jnp.bfloat16)],
        in_specs=[SMEM, SMEM, VMEM, VMEM, SMEM, VMEM, HBM, HBM],
        out_specs=[VMEM, VMEM, VMEM],
        scratch_shapes=[
            pltpu.VMEM((ENTRIES, BLOCK_ROWS, B, B), jnp.bfloat16),
            pltpu.VMEM((ENTRIES, ROWS // 2, B), jnp.bfloat16),
            pltpu.VMEM((NCOL, 2 * B, ROWS), jnp.bfloat16),
            pltpu.VMEM((ENTRIES, B, ROWS), jnp.bfloat16),
            pltpu.VMEM((GATHER_ROUNDS, ENTRIES * GATHER_ROWS, WIDTH), jnp.bfloat16),
            pltpu.VMEM((GROUPS * B, 2 * B), jnp.bfloat16),
            pltpu.VMEM((RETURN_ROUNDS, ENTRIES, ENTRIES, RETURN_ROWS, B), jnp.bfloat16),
            pltpu.VMEM((8, ROWS), jnp.float32),
            pltpu.VMEM((1, ROWS), jnp.float32),
            [pltpu.VMEM(parts, jnp.bfloat16)] * RETURN_ROUNDS,
            [pltpu.VMEM(parts, jnp.bfloat16)] * RETURN_ROUNDS,
            pltpu.VMEM((GROUPS, RUN, B), jnp.float32),
            pltpu.VMEM(slots, jnp.bfloat16),
            pltpu.VMEM(slots, jnp.bfloat16),
            pltpu.SMEM((2, GROUPS), jnp.float32),
            pltpu.VMEM((8, GROUPS), jnp.int32),
            pltpu.SMEM((8, GROUPS), jnp.int32),
            dma, dma, dma, dma, dma((GATHER_ROUNDS,)), dma, dma((RETURN_ROUNDS,)), dma, dma((RETURN_ROUNDS,)), dma,
        ] + [dma((RETURN_ROUNDS, SLOTS))] * 4,
        compiler_params=pltpu.CompilerParams(
            collective_id=0, has_side_effects=True, vmem_limit_bytes=61 << 20
        ),
        cost_estimate=pl.CostEstimate(flops=4 * ROWS * WIDTH * WIDTH, bytes_accessed=16 << 20, transcendentals=2 * ROWS),
    )(lists, home, lists, home.reshape(1, GROUPS), cnt, w, dens, phi)


def place_kernel(near_hbm, wide_hbm, mirrored_hbm, out_hbm, near_ref, wide_ref, mirrored_ref, rows_ref, in_sem, out_sem):
    row, col = lax.axis_index("row"), lax.axis_index("col")
    shift = lag(row, col)
    near_copy = pltpu.make_async_copy(near_hbm, near_ref, in_sem.at[0])
    wide_copy = pltpu.make_async_copy(wide_hbm, wide_ref, in_sem.at[1])
    mirrored_copy = pltpu.make_async_copy(mirrored_hbm, mirrored_ref, in_sem.at[2])
    for copy in (near_copy, wide_copy, mirrored_copy):
        copy.start()

    def clear(i, carry):
        rows_ref[i] = jnp.zeros((B, WIDTH), jnp.float32)
        return carry

    lax.fori_loop(0, BLOCK_ROWS, clear, 0)
    for copy in (near_copy, wide_copy, mirrored_copy):
        copy.wait()

    def columns(q):
        return pl.ds(pl.multiple_of(((q & (GROUPS - 1)) >> 3) * B, B), B)

    def out_copy(i):
        return pltpu.make_async_copy(rows_ref.at[i], out_hbm.at[i], out_sem.at[i])

    def fill(i, carry):
        p = row + NROW * i

        @pl.when(shift == 0)
        def _():
            rows_ref[i, :, columns(p)] = near_ref[i * 2]

        @pl.when(shift != 0)
        def _():
            for w in range(2):
                rows_ref[i, :, columns(p + shift - NROW * w)] = near_ref[i * 2 + w]

        @pl.when(keeps_far(row, col))
        def _():
            for w in range(2):
                rows_ref[i, :, columns(p + NCOL - NROW * w)] = wide_ref[i * 2 + w]

        @pl.when(jnp.logical_not(keeps_far(row, col)))
        def _():
            for w in range(2):
                there = p - (NCOL - shift) + NROW * w
                at = ((there & (GROUPS - 1)) >> 4) * 2 + w
                block = jnp.concatenate([mirrored_ref[n, at] for n in range(RETURN_ROUNDS)], axis=0)
                rows_ref[i, :, columns(there)] = block.astype(jnp.float32).T

        out_copy(i).start()
        return carry

    lax.fori_loop(0, BLOCK_ROWS, fill, 0)

    def drain(i, carry):
        out_copy(i).wait()
        return carry

    lax.fori_loop(0, BLOCK_ROWS, drain, 0)


def assemble(near, wide, mirrored):
    return pl.pallas_call(
        place_kernel,
        out_shape=jax.ShapeDtypeStruct((BLOCK_ROWS, B, WIDTH), jnp.float32),
        in_specs=[HBM] * 3,
        out_specs=HBM,
        scratch_shapes=[
            pltpu.VMEM((SLOTS, B, B), jnp.float32),
            pltpu.VMEM((SLOTS, B, B), jnp.float32),
            pltpu.VMEM((RETURN_ROUNDS, SLOTS, RETURN_ROWS, B), jnp.bfloat16),
            pltpu.VMEM((BLOCK_ROWS, B, WIDTH), jnp.float32),
            pltpu.SemaphoreType.DMA((3,)),
            pltpu.SemaphoreType.DMA((BLOCK_ROWS,)),
        ],
        compiler_params=pltpu.CompilerParams(vmem_limit_bytes=62 << 20),
    )(near, wide, mirrored).reshape(BLOCK_ROWS * B, WIDTH)


def body(basis_values, point_weights, density_stored, relevant_blocks, relevant_count, block_home):
    near, wide, mirrored = exchange(
        relevant_blocks.T, block_home, relevant_count, point_weights,
        density_stored.reshape(BLOCK_ROWS, B, WIDTH), basis_values,
    )
    return assemble(near, wide, mirrored)


def solution(mesh):
    in_specs = (P(("row", "col"), None), P(("row", "col")), P("row", "col"), P(), P(), P())
    return jax.shard_map(body, mesh=mesh, in_specs=in_specs, out_specs=P("row", "col"), check_vma=False)
```

```python
import jax
import jax.numpy as jnp
from jax import lax
from jax.experimental import pallas as pl
from jax.experimental.pallas import tpu as pltpu
from jax.sharding import PartitionSpec as P

MESH = pl.DeviceIdType.MESH
NROW, NCOL, GROUPS, B = 16, 8, 128, 128
ENTRIES = 16
ROWS = 1536
WIDTH = ENTRIES * B
BLOCK_ROWS = 8
GATHER_ROUNDS, GATHER_ROWS = 8, 16
RETURN_ROUNDS, RETURN_ROWS = 2, 64
RUN = 32
SLOTS = 2 * BLOCK_ROWS


def place(residue):
    return (residue % NCOL) * 2 + residue // NCOL


def offset_target(step, row, col):
    t = (step * (step + 1) // 2) % GROUPS
    y = (row // 4 + t % 4) % 4
    x = (row % 4 + (t // 4) % 4) % 4
    z = (col // 2 + (t // 16) % 4) % 4
    core = (col + t // 64) % 2
    return y * 4 + x, z * 2 + core


def list_place(start, residue):
    return (residue - start) & (ENTRIES - 1)


def position(start, residue):
    return (start + list_place(start, residue)) & (GROUPS - 1)


def lag(row, col):
    return (col - row + NROW) % NCOL


def keeps_far(row, col):
    return (lag(row, col) == 0) & (row < NCOL)


def mirror_owner(row, col):
    shift = lag(row, col)
    return (row + shift + NCOL * (shift == 0).astype(jnp.int32)) % NROW, row % NCOL


def group_kernel(
    first_ref, home_ref, first_row, home_row, cnt_ref, w_ref, dens_hbm, phi_hbm, near_ref, wide_ref, mirrored_ref,
    dens_ref, phi_ref, scaled_ref, phit_ref, sub_ref, stage_ref, back_ref, rho_ref, pot_ref,
    main_refs, far_refs, run_ref, turned_ref, relay_ref, keep_ref, table_ref, order_ref,
    table_sem, dens_sem, phi_sem, dsend, drecv, msend, mrecv, fsend, frecv, self_sem, send1, recv1, send2, recv2,
):
    row, col = lax.axis_index("row"), lax.axis_index("col")
    me = row * NCOL + col

    def start_of(group):
        return home_ref[first_ref[0, group]]

    def column(k):
        return pl.ds(k * B, B)

    dens_copies = [
        pltpu.make_async_copy(dens_hbm.at[:, :, column(k)], dens_ref.at[k], dens_sem) for k in range(ENTRIES)
    ]
    for copy in dens_copies:
        copy.start()

    def load_phi(half):
        for k in range(ENTRIES):
            pltpu.make_async_copy(
                phi_hbm.at[pl.ds(half * (ROWS // 2), ROWS // 2), column(k)], phi_ref.at[k], phi_sem
            ).start()

    load_phi(0)

    barrier = pltpu.get_barrier_semaphore()

    def greet(i, carry):
        r, c = offset_target(i, row, col)
        pl.semaphore_signal(barrier, inc=1, device_id=(r, c), device_id_type=MESH)
        return carry

    lax.fori_loop(1, GROUPS, greet, 0)

    def pick(r, c):
        start = start_of(r * NCOL + c)
        i = position(start, row) >> 4
        j0 = position(start, col) >> 3
        j1 = position(start, col + NCOL) >> 3
        return dens_ref[j0, i], dens_ref[j1, i]

    pltpu.make_async_copy(dens_ref, dens_ref, dens_sem).wait()

    def staged(n, r, c):
        at = (n * GROUPS + r * NCOL + c) * GATHER_ROWS
        return pl.ds(pl.multiple_of(at, GATHER_ROWS), GATHER_ROWS)

    def prepare(i, carry):
        r, c = offset_target(i, row, col)
        left, right = pick(r, c)
        for n in range(GATHER_ROUNDS):
            part = slice(n * GATHER_ROWS, (n + 1) * GATHER_ROWS)
            stage_ref[staged(n, r, c), pl.ds(0, B)] = left[part]
            stage_ref[staged(n, r, c), pl.ds(B, B)] = right[part]
        return carry

    lax.fori_loop(1, GROUPS, prepare, 0, unroll=2)
    my_rows = pl.ds(pl.multiple_of(place(row) * GATHER_ROWS, GATHER_ROWS), GATHER_ROWS)
    my_cols = pl.ds(pl.multiple_of(col * 2 * B, B), 2 * B)
    left, right = pick(row, col)
    for n in range(GATHER_ROUNDS):
        part = slice(n * GATHER_ROWS, (n + 1) * GATHER_ROWS)
        sub_ref[n, my_rows, my_cols] = jnp.concatenate([left[part], right[part]], axis=1)

    pl.semaphore_wait(barrier, GROUPS - 1)

    def send_round(n, carry):
        def send(i, carry):
            r, c = offset_target(i, row, col)
            pltpu.make_async_remote_copy(
                src_ref=stage_ref.at[staged(n, r, c)],
                dst_ref=sub_ref.at[n, my_rows, my_cols],
                send_sem=dsend, recv_sem=drecv.at[n],
                device_id=(r, c), device_id_type=MESH,
            ).start()
            return carry

        return lax.fori_loop(1, GROUPS, send, carry, unroll=2)

    lax.fori_loop(0, GATHER_ROUNDS, send_round, 0)

    my_start = start_of(me)
    my_count = cnt_ref[me]

    for half in range(2):
        pltpu.make_async_copy(phi_ref, phi_ref, phi_sem).wait()

        def turn(at, carry):
            residue = at // 2 + (at % 2) * NCOL
            k = list_place(my_start, residue)
            live = jnp.clip(my_count - k, 0, 1).astype(jnp.float32)
            for t in range(ROWS // 2 // B):
                tile = phi_ref[k, pl.ds(t * B, B), :]
                tile = (tile.astype(jnp.float32) * live).T
                phit_ref[at, :, pl.ds(half * (ROWS // 2) + t * B, B)] = tile.astype(jnp.bfloat16)
            return carry

        lax.fori_loop(0, ENTRIES, turn, 0)
        if half == 0:
            load_phi(1)

    shift = lag(row, col)

    lane = lax.broadcasted_iota(jnp.int32, (GROUPS, GROUPS), 1)
    line = lax.broadcasted_iota(jnp.int32, (GROUPS, GROUPS), 0)
    homes = jnp.broadcast_to(home_row[...], (GROUPS, GROUPS)).T
    starts = jnp.sum(jnp.where(first_row[0:1, :] == line, homes, 0), axis=0, keepdims=True)
    across = jnp.broadcast_to(starts, (GROUPS, GROUPS))
    down = across.T
    ahead = ((across < down) | ((across == down) & (lane < line))).astype(jnp.int32)
    rank = jnp.sum(ahead, axis=1, keepdims=True)
    table_ref[0:1, :] = jnp.sum(jnp.where(rank == lane, line, 0), axis=0, keepdims=True)
    table_ref[1:2, :] = jnp.sum((down < lane).astype(jnp.int32), axis=0, keepdims=True)
    table_ref[2:3, :] = jnp.sum((down < lane + GROUPS).astype(jnp.int32), axis=0, keepdims=True)
    table_ref[3:4, :] = jnp.sum(jnp.where(rank == lane, down, 0), axis=0, keepdims=True)
    tables = pltpu.make_async_copy(table_ref, order_ref, table_sem)
    tables.start()
    tables.wait()

    def below(at):
        return order_ref[1 + at // GROUPS, at % GROUPS]

    def segment(start, apart):
        k = list_place(start, row)
        whole = jnp.clip(ENTRIES - apart - k, 0, 1)
        return ((start + k) >> 4) * 2 + whole

    def keeps(m, carry):
        for at, apart in ((0, shift), (1, NCOL)):
            same = 1 - jnp.clip(segment(order_ref[3, m], apart) - segment(order_ref[3, m - 1], apart), 0, 1)
            keep_ref[at, m] = same.astype(jnp.float32)
        return carry

    keep_ref[0, 0] = 0.0
    keep_ref[1, 0] = 0.0
    lax.fori_loop(1, GROUPS, keeps, 0)
    rho_ref[...] = jnp.zeros_like(rho_ref)

    M, N = ENTRIES * GATHER_ROWS, 256
    one_round = stage_ref.at[pl.ds(0, (GROUPS - 1) * GATHER_ROWS)]

    def density_round(n, carry):
        pltpu.make_async_copy(one_round, one_round, drecv.at[n]).wait()
        rows = pl.ds(pl.multiple_of(n * GATHER_ROWS, GATHER_ROWS), GATHER_ROWS)

        def density(step, carry):
            cols = pl.ds(pl.multiple_of(step * N, N), N)
            g = jnp.dot(
                sub_ref[n], phit_ref[:, :, cols].reshape(WIDTH, N), preferred_element_type=jnp.float32
            )
            g = g * phit_ref[:, rows, cols].reshape(M, N).astype(jnp.float32)
            rho_ref[:, cols] += jnp.sum(g.reshape(M // 8, 8, N), axis=0)
            return carry

        return lax.fori_loop(0, ROWS // N, density, carry)

    lax.fori_loop(0, GATHER_ROUNDS, density_round, 0)

    rho = jnp.sum(rho_ref[...], axis=0, keepdims=True)
    pot_ref[...] = w_ref[...].reshape(1, ROWS) * rho * jnp.exp(jnp.log(1.0 + rho * rho) * (-1.0 / 3.0))

    def weigh(c, carry):
        scaled_ref[c] = (
            phit_ref[pl.ds(c * 2, 2)].reshape(2 * B, ROWS).astype(jnp.float32) * pot_ref[...]
        ).astype(jnp.bfloat16)
        return carry

    lax.fori_loop(0, NCOL, weigh, 0)

    HALF = ENTRIES // 2

    def return_round(n):
        rows = pl.ds(pl.multiple_of(n * RETURN_ROWS, RETURN_ROWS), RETURN_ROWS)

        def potential(step, carry):
            c, half = step // 2, step % 2
            v = lax.dot_general(
                phit_ref[pl.ds(half * HALF, HALF), rows, :].reshape(HALF * RETURN_ROWS, ROWS), scaled_ref[c],
                (((1,), (1,)), ((), ())), preferred_element_type=jnp.float32,
            ).astype(jnp.bfloat16).reshape(HALF, RETURN_ROWS, 2 * B)
            back_ref[n, c * 2, pl.ds(half * HALF, HALF)] = v[:, :, :B]
            back_ref[n, c * 2 + 1, pl.ds(half * HALF, HALF)] = v[:, :, B:]
            return carry

        lax.fori_loop(0, NCOL * 2, potential, 0)

        def main_copy(r, c):
            residue = (r + lag(r, c)) % NROW
            return pltpu.make_async_remote_copy(
                src_ref=back_ref.at[n, place(residue), place(r)],
                dst_ref=main_refs[n].at[me],
                send_sem=msend, recv_sem=mrecv.at[n],
                device_id=(r, c), device_id_type=MESH,
            )

        def far_copy(r, c):
            residue = (r + NCOL) % NROW
            return pltpu.make_async_remote_copy(
                src_ref=back_ref.at[n, place(residue), place(r)],
                dst_ref=far_refs[n].at[me],
                send_sem=fsend, recv_sem=frecv.at[n],
                device_id=(r, c), device_id_type=MESH,
            )

        def give(i, carry):
            r, c = offset_target(i, row, col)
            main_copy(r, c).start()

            @pl.when(keeps_far(r, c))
            def _():
                far_copy(r, c).start()

            return carry

        lax.fori_loop(1, GROUPS, give, 0, unroll=2)
        residue = (row + lag(row, col)) % NROW
        own = pltpu.make_async_copy(back_ref.at[n, place(residue), place(row)], main_refs[n].at[me], self_sem)
        own.start()
        own.wait()

        @pl.when(keeps_far(row, col))
        def _():
            residue = (row + NCOL) % NROW
            own = pltpu.make_async_copy(back_ref.at[n, place(residue), place(row)], far_refs[n].at[me], self_sem)
            own.start()
            own.wait()

    for n in range(RETURN_ROUNDS):
        return_round(n)
    gathered = stage_ref.at[pl.ds(0, (GROUPS - 1) * B)]
    pltpu.make_async_copy(gathered, gathered, dsend).wait()

    def relay_shift(i):
        return (5 * i + 1) % NROW, (3 * i) % NCOL

    def relay(i):
        dr, dc = relay_shift(i)
        return (row + dr) % NROW, (col + dc) % NCOL

    def final(i):
        dr, dc = relay_shift(i)
        return mirror_owner((row - dr + NROW) % NROW, (col - dc + NCOL) % NCOL)

    def first(n, i):
        return pltpu.make_async_remote_copy(
            src_ref=turned_ref.at[n, i], dst_ref=relay_ref.at[n, i], send_sem=send1.at[n, i], recv_sem=recv1.at[n, i],
            device_id=relay(i), device_id_type=MESH,
        )

    def second(n, i):
        return pltpu.make_async_remote_copy(
            src_ref=relay_ref.at[n, i], dst_ref=mirrored_ref.at[n, i], send_sem=send2.at[n, i], recv_sem=recv2.at[n, i],
            device_id=final(i), device_id_type=MESH,
        )

    def stays(i):
        r, c = final(i)
        return r * NCOL + c == me

    def total(parts_ref, n, which, apart, out_ref):
        for u in range(RETURN_ROWS // RUN):
            rows = pl.ds(u * RUN, RUN)

            def add(m, acc):
                acc = acc * keep_ref[which, m] + parts_ref[order_ref[0, m], rows, :].astype(jnp.float32)
                run_ref[m] = acc
                return acc

            lax.fori_loop(0, GROUPS, add, jnp.zeros((RUN, B), jnp.float32), unroll=8)
            out_rows = pl.ds(pl.multiple_of(n * RETURN_ROWS + u * RUN, RUN), RUN)

            def slot(at, carry):
                i, w = at // 2, at % 2

                def ended(i):
                    p = row + i * NROW
                    low = jnp.where(w == 1, p - 15, p - 15 + apart)
                    high = jnp.where(w == 1, p - 15 + apart, p + 1)
                    before = below(jnp.clip(low, 0, GROUPS))
                    until = below(jnp.clip(high, 0, GROUPS))
                    some = jnp.clip(until - before, 0, 1).astype(jnp.float32)
                    return run_ref[jnp.maximum(until - 1, 0)] * some

                out_ref[at, out_rows, :] = ended(i)

                @pl.when(i == 0)
                def _():
                    out_ref[at, out_rows, :] += ended(BLOCK_ROWS)

                return carry

            lax.fori_loop(0, SLOTS, slot, 0)

    one_part = stage_ref.at[pl.ds(0, (GROUPS - 1) * RETURN_ROWS // 2)]

    def finish_round(n):
        def total_near():
            pltpu.make_async_copy(one_part, one_part, mrecv.at[n]).wait()
            total(main_refs[n], n, 0, shift, near_ref)

        pl.when(jnp.logical_not(keeps_far(row, col)))(total_near)

        @pl.when(keeps_far(row, col))
        def _():
            pltpu.make_async_copy(one_part, one_part, frecv.at[n]).wait()
            total(far_refs[n], n, 1, NCOL, wide_ref)

        def start_first(i, carry):
            rows = pl.ds(pl.multiple_of(n * RETURN_ROWS, RETURN_ROWS), RETURN_ROWS)

            @pl.when(keeps_far(row, col))
            def _():
                turned_ref[n, i] = wide_ref[i, rows, :].astype(jnp.bfloat16)

            @pl.when(jnp.logical_not(keeps_far(row, col)))
            def _():
                turned_ref[n, i] = near_ref[i, rows, :].astype(jnp.bfloat16)

            first(n, i).start()
            return carry

        lax.fori_loop(0, SLOTS, start_first, 0)

        def pass_on(i, carry):
            first(n, i).wait_recv()

            @pl.when(jnp.logical_not(stays(i)))
            def _():
                second(n, i).start()

            @pl.when(stays(i))
            def _():
                pltpu.make_async_copy(relay_ref.at[n, i], mirrored_ref.at[n, i], recv2.at[n, i]).start()

            return carry

        lax.fori_loop(0, SLOTS, pass_on, 0)
        pl.when(keeps_far(row, col))(total_near)

    @pl.when(jnp.logical_not(keeps_far(row, col)))
    def _():
        wide_ref[...] = jnp.zeros_like(wide_ref)

    for n in range(RETURN_ROUNDS):
        finish_round(n)

    def done(at, carry):
        n, i = at // SLOTS, at % SLOTS
        first(n, i).wait_send()
        second(n, i).wait_recv()

        @pl.when(jnp.logical_not(stays(i)))
        def _():
            second(n, i).wait_send()

        return carry

    lax.fori_loop(0, RETURN_ROUNDS * SLOTS, done, 0)

    sent = stage_ref.at[pl.ds(0, (GROUPS - 1) * B // 2)]
    pltpu.make_async_copy(sent, sent, msend).wait()

    @pl.when(keeps_far(row, col))
    def _():
        others = stage_ref.at[pl.ds(0, (NCOL - 1) * B // 2)]
        pltpu.make_async_copy(others, others, fsend).wait()

    @pl.when(jnp.logical_not(keeps_far(row, col)))
    def _():
        others = stage_ref.at[pl.ds(0, NCOL * B // 2)]
        pltpu.make_async_copy(others, others, fsend).wait()


VMEM = pl.BlockSpec(memory_space=pltpu.VMEM)
SMEM = pl.BlockSpec(memory_space=pltpu.SMEM)
HBM = pl.BlockSpec(memory_space=pl.ANY)


def exchange(lists, home, cnt, w, dens, phi):
    sums = jax.ShapeDtypeStruct((SLOTS, B, B), jnp.float32)
    parts = (GROUPS, RETURN_ROWS, B)
    slots = (RETURN_ROUNDS, SLOTS, RETURN_ROWS, B)
    dma = pltpu.SemaphoreType.DMA
    return pl.pallas_call(
        group_kernel,
        out_shape=[sums, sums, jax.ShapeDtypeStruct(slots, jnp.bfloat16)],
        in_specs=[SMEM, SMEM, VMEM, VMEM, SMEM, VMEM, HBM, HBM],
        out_specs=[VMEM, VMEM, VMEM],
        scratch_shapes=[
            pltpu.VMEM((ENTRIES, BLOCK_ROWS, B, B), jnp.bfloat16),
            pltpu.VMEM((ENTRIES, ROWS // 2, B), jnp.bfloat16),
            pltpu.VMEM((NCOL, 2 * B, ROWS), jnp.bfloat16),
            pltpu.VMEM((ENTRIES, B, ROWS), jnp.bfloat16),
            pltpu.VMEM((GATHER_ROUNDS, ENTRIES * GATHER_ROWS, WIDTH), jnp.bfloat16),
            pltpu.VMEM((GROUPS * B, 2 * B), jnp.bfloat16),
            pltpu.VMEM((RETURN_ROUNDS, ENTRIES, ENTRIES, RETURN_ROWS, B), jnp.bfloat16),
            pltpu.VMEM((8, ROWS), jnp.float32),
            pltpu.VMEM((1, ROWS), jnp.float32),
            [pltpu.VMEM(parts, jnp.bfloat16)] * RETURN_ROUNDS,
            [pltpu.VMEM(parts, jnp.bfloat16)] * RETURN_ROUNDS,
            pltpu.VMEM((GROUPS, RUN, B), jnp.float32),
            pltpu.VMEM(slots, jnp.bfloat16),
            pltpu.VMEM(slots, jnp.bfloat16),
            pltpu.SMEM((2, GROUPS), jnp.float32),
            pltpu.VMEM((8, GROUPS), jnp.int32),
            pltpu.SMEM((8, GROUPS), jnp.int32),
            dma, dma, dma, dma, dma((GATHER_ROUNDS,)), dma, dma((RETURN_ROUNDS,)), dma, dma((RETURN_ROUNDS,)), dma,
        ] + [dma((RETURN_ROUNDS, SLOTS))] * 4,
        compiler_params=pltpu.CompilerParams(
            collective_id=0, has_side_effects=True, vmem_limit_bytes=61 << 20
        ),
        cost_estimate=pl.CostEstimate(flops=4 * ROWS * WIDTH * WIDTH, bytes_accessed=16 << 20, transcendentals=2 * ROWS),
    )(lists, home, lists, home.reshape(1, GROUPS), cnt, w, dens, phi)


def place_kernel(near_hbm, wide_hbm, mirrored_hbm, out_hbm, near_ref, wide_ref, mirrored_ref, rows_ref, in_sem, out_sem):
    row, col = lax.axis_index("row"), lax.axis_index("col")
    shift = lag(row, col)
    near_copy = pltpu.make_async_copy(near_hbm, near_ref, in_sem.at[0])
    wide_copy = pltpu.make_async_copy(wide_hbm, wide_ref, in_sem.at[1])
    mirrored_copy = pltpu.make_async_copy(mirrored_hbm, mirrored_ref, in_sem.at[2])
    for copy in (near_copy, wide_copy, mirrored_copy):
        copy.start()

    def clear(i, carry):
        rows_ref[i] = jnp.zeros((B, WIDTH), jnp.float32)
        return carry

    lax.fori_loop(0, BLOCK_ROWS, clear, 0)
    for copy in (near_copy, wide_copy, mirrored_copy):
        copy.wait()

    def columns(q):
        return pl.ds(pl.multiple_of(((q & (GROUPS - 1)) >> 3) * B, B), B)

    def out_copy(i):
        return pltpu.make_async_copy(rows_ref.at[i], out_hbm.at[i], out_sem.at[i])

    def fill(i, carry):
        p = row + NROW * i

        @pl.when(shift == 0)
        def _():
            rows_ref[i, :, columns(p)] = near_ref[i * 2]

        @pl.when(shift != 0)
        def _():
            for w in range(2):
                rows_ref[i, :, columns(p + shift - NROW * w)] = near_ref[i * 2 + w]

        @pl.when(keeps_far(row, col))
        def _():
            for w in range(2):
                rows_ref[i, :, columns(p + NCOL - NROW * w)] = wide_ref[i * 2 + w]

        @pl.when(jnp.logical_not(keeps_far(row, col)))
        def _():
            for w in range(2):
                there = p - (NCOL - shift) + NROW * w
                at = ((there & (GROUPS - 1)) >> 4) * 2 + w
                block = jnp.concatenate([mirrored_ref[n, at] for n in range(RETURN_ROUNDS)], axis=0)
                rows_ref[i, :, columns(there)] = block.astype(jnp.float32).T

        out_copy(i).start()
        return carry

    lax.fori_loop(0, BLOCK_ROWS, fill, 0)

    def drain(i, carry):
        out_copy(i).wait()
        return carry

    lax.fori_loop(0, BLOCK_ROWS, drain, 0)


def assemble(near, wide, mirrored):
    return pl.pallas_call(
        place_kernel,
        out_shape=jax.ShapeDtypeStruct((BLOCK_ROWS, B, WIDTH), jnp.float32),
        in_specs=[HBM] * 3,
        out_specs=HBM,
        scratch_shapes=[
            pltpu.VMEM((SLOTS, B, B), jnp.float32),
            pltpu.VMEM((SLOTS, B, B), jnp.float32),
            pltpu.VMEM((RETURN_ROUNDS, SLOTS, RETURN_ROWS, B), jnp.bfloat16),
            pltpu.VMEM((BLOCK_ROWS, B, WIDTH), jnp.float32),
            pltpu.SemaphoreType.DMA((3,)),
            pltpu.SemaphoreType.DMA((BLOCK_ROWS,)),
        ],
        compiler_params=pltpu.CompilerParams(vmem_limit_bytes=62 << 20),
    )(near, wide, mirrored).reshape(BLOCK_ROWS * B, WIDTH)


def body(basis_values, point_weights, density_stored, relevant_blocks, relevant_count, block_home):
    near, wide, mirrored = exchange(
        relevant_blocks.T, block_home, relevant_count, point_weights,
        density_stored.reshape(BLOCK_ROWS, B, WIDTH), basis_values,
    )
    return assemble(near, wide, mirrored)


def solution(mesh):
    in_specs = (P(("row", "col"), None), P(("row", "col")), P("row", "col"), P(), P(), P())
    return jax.shard_map(body, mesh=mesh, in_specs=in_specs, out_specs=P("row", "col"), check_vma=False)
```
